32 devices in a mesh: ctx: 2 (over x), head: 4 (over y, core), clip: 4 (over z).
Axes of the slice: x: 2, y: 2, z: 4, core: 2. Of those that a mesh axis runs over, the one named last changes fastest.
Arguments:
- queries: bfloat16 [4, 256, 2560], P('clip', 'ctx', 'head'), may hold values from -40 to 40
- key_states: bfloat16 [4, 256, 2560], P('clip', 'ctx', 'head'), may hold values from -40 to 40
- value_states: bfloat16 [4, 256, 2560], P('clip', 'ctx', 'head'), may hold values from -40 to 40
- layer_grad: bfloat16 [4, 256, 5120], P('clip', 'ctx'), may hold values from -6 to 6
- out_weight: bfloat16 [2560, 5120], P('head', 'clip'), may hold values from -0.125 to 0.125
- chosen: int32 [4, 4, 2], P('clip', 'ctx'), may hold values from 0 to 3, all different within a row
Outputs:
- attention: bfloat16 [4, 256, 2560], P('clip', 'ctx', 'head')
- query_grad: bfloat16 [4, 256, 2560], P('clip', 'ctx', 'head')
- key_grad: bfloat16 [4, 256, 2560], P('clip', 'ctx', 'head')
- value_grad: bfloat16 [4, 256, 2560], P('clip', 'ctx', 'head')
- weight_grad: bfloat16 [2560, 5120], P('head', 'clip')
The draws below stay inside these ranges and needn't reach their ends.
Inputs may be any that keep to these rules, and one draw needn't show every extreme that they name: Each row names 2 different cubes of its clip; how often a key cube is chosen differs widely from cube to cube.
All inputs are finite; a program needn't handle non-finite values.
Results may differ from the reference program's by a relative error of at most 0.025.
Values may be sent and summed in bfloat16 or wider, within the bound.
A program may use at most 128 MiB of HBM per device.

```python
import jax
import jax.numpy as jnp
from jax import lax

D = 5120
HD = 128
CUBE = 64
CUBES_DEV = 2
HEADS = 20
NC = 4
TOKENS = 256
TOPK = 2
CLIPS = 4
N_CTX = 2


def cube_field(key, salt):
    field = jax.random.normal(jax.random.fold_in(key, salt), (CLIPS, NC, 1, HEADS * HD), jnp.float32)
    return jnp.broadcast_to(field, (CLIPS, NC, CUBE, HEADS * HD)).reshape(CLIPS, TOKENS, HEADS * HD)


def draw_queries(key, part):
    noise_key = jax.random.fold_in(key, 1)
    drawn = jax.random.normal(noise_key, (CLIPS, TOKENS, HEADS * HD), jnp.float32) + cube_field(key, 211)
    return jnp.clip(drawn, -40.0, 40.0).astype(jnp.bfloat16)


def draw_key_states(key, part):
    noise_key = jax.random.fold_in(key, 2)
    drawn = jax.random.normal(noise_key, (CLIPS, TOKENS, HEADS * HD), jnp.float32) + cube_field(key, 223)
    return jnp.clip(drawn, -40.0, 40.0).astype(jnp.bfloat16)


def draw_value_states(key, part):
    noise_key = jax.random.fold_in(key, 4)
    drawn = jax.random.normal(noise_key, (CLIPS, TOKENS, HEADS * HD), jnp.float32) + cube_field(key, 227)
    return jnp.clip(drawn, -40.0, 40.0).astype(jnp.bfloat16)


def shard_levels(key, shape, cuts, least, high):
    def one(axis_at, shards_of):
        heights = jax.random.uniform(jax.random.fold_in(jax.random.fold_in(key, 6), axis_at), (shards_of,), jnp.float32, least / len(cuts), high / len(cuts))
        return jnp.repeat(jnp.exp(heights), shape[axis_at] // shards_of).reshape((-1,) + (1,) * (len(shape) - axis_at - 1))

    loudness = one(*cuts[0])
    for cut in cuts[1:]:
        loudness = loudness * one(*cut)
    return loudness


def picks_of(stream_key, rows, number_of, top, lift):
    ranking = jax.random.permutation(jax.random.fold_in(stream_key, 1), number_of)
    boost = ranking
    for power in range(3):
        boost = boost * boost // number_of
    boost = boost * lift // number_of
    chance = jax.random.randint(jax.random.fold_in(stream_key, 2), (rows, number_of), 0, 4096) + boost
    holders = jax.random.permutation(jax.random.fold_in(stream_key, 3), rows)[jnp.arange(number_of) % rows]
    chance = jnp.where(jnp.arange(rows)[:, None] == holders[None, :], 1 << 14, chance)
    priority = chance * number_of + jnp.arange(number_of)
    return lax.top_k(priority.astype(jnp.int32), top)[1].astype(jnp.int32)


def normal_values(own_key, extent, spread, reach, pieces=(), held_as=jnp.bfloat16):
    result = spread * jax.random.normal(own_key, extent, jnp.float32)
    if pieces:
        result = result * shard_levels(own_key, extent, pieces, -0.22, 0.18)
    return jnp.clip(result, -reach, reach).astype(held_as)


def setup_inputs(seed: int = 0) -> dict:
    splits = jax.random.split(jax.random.key(seed), 7)
    return {
        "queries": draw_queries(jax.random.fold_in(splits[6], 71), 0),
        "key_states": draw_key_states(jax.random.fold_in(splits[6], 71), 0),
        "value_states": draw_value_states(jax.random.fold_in(splits[6], 71), 0),
        "layer_grad": normal_values(splits[3], (CLIPS, TOKENS, D), 1.0, 6.0, ((0, 4), (1, 2))),
        "out_weight": normal_values(splits[4], (HEADS * HD, D), (HEADS * HD) ** -0.5, 0.125, ((0, 4), (1, 4))),
        "chosen": picks_of(splits[5], CLIPS * NC, NC, TOPK, 8192).reshape((CLIPS, NC, TOPK)),
    }


def pooled(blocks):
    grouped = blocks.astype(jnp.float32).reshape(-1, CUBE, blocks.shape[-1])
    return jnp.mean(grouped, axis=1).astype(jnp.bfloat16)


def softmax_rows(scores):
    largest = jnp.max(scores, axis=-1, keepdims=True)
    expons = jnp.exp(scores - largest)
    return expons / jnp.sum(expons, axis=-1, keepdims=True)


def group_sum(picked_terms, coarse_weights, coarse_inputs, chosen_group):
    running = jnp.zeros((NC, CUBE, HD), jnp.float32)
    running = running.at[chosen_group.reshape(-1)].add(picked_terms.reshape(-1, CUBE, HD))
    cube_term = jnp.dot(coarse_weights.T.astype(jnp.float32), coarse_inputs.astype(jnp.float32))
    rounded = lax.optimization_barrier((running + cube_term[:, None, :] / CUBE).astype(jnp.bfloat16))
    return rounded.astype(jnp.float32)


def one_head(inputs):
    query_rows, key_rows, value_rows, grad_rows, chosen_rows = inputs
    scaling = HD ** -0.5
    q_cube = pooled(query_rows)
    k_cube = pooled(key_rows)
    v_cube = pooled(value_rows)
    coarse_p = softmax_rows(jnp.dot(q_cube, k_cube.T, preferred_element_type=jnp.float32) * scaling)
    coarse_half = coarse_p.astype(jnp.bfloat16)
    coarse_out = jnp.dot(coarse_half, v_cube, preferred_element_type=jnp.float32)
    query_blocks = query_rows.reshape(NC, CUBE, HD).astype(jnp.float32)
    grad_blocks = grad_rows.reshape(NC, CUBE, HD).astype(jnp.float32)
    key_pick = key_rows.reshape(NC, CUBE, HD)[chosen_rows].reshape(NC, TOPK * CUBE, HD).astype(jnp.float32)
    value_pick = value_rows.reshape(NC, CUBE, HD)[chosen_rows].reshape(NC, TOPK * CUBE, HD).astype(jnp.float32)
    fine_p = softmax_rows(jnp.einsum("ctd,ckd->ctk", query_blocks, key_pick) * scaling)
    fine_half = fine_p.astype(jnp.bfloat16)
    fine_out = jnp.einsum("ctk,ckd->ctd", fine_half.astype(jnp.float32), value_pick)
    attention = (fine_out + coarse_out[:, None, :]).astype(jnp.bfloat16).reshape(TOKENS, HD)
    grad_cube = jnp.sum(grad_blocks, axis=1).astype(jnp.bfloat16)
    coarse_dp = jnp.dot(grad_cube, v_cube.T, preferred_element_type=jnp.float32)
    coarse_delta = jnp.sum(coarse_p * coarse_dp, axis=-1, keepdims=True)
    coarse_ds = (scaling * coarse_p * (coarse_dp - coarse_delta)).astype(jnp.bfloat16)
    coarse_dq = jnp.dot(coarse_ds, k_cube, preferred_element_type=jnp.float32)
    fine_dp = jnp.einsum("ctd,ckd->ctk", grad_blocks, value_pick)
    fine_delta = jnp.sum(fine_p * fine_dp, axis=-1, keepdims=True)
    fine_ds = (scaling * fine_p * (fine_dp - fine_delta)).astype(jnp.bfloat16)
    query_grad = jnp.einsum("ctk,ckd->ctd", fine_ds.astype(jnp.float32), key_pick) + coarse_dq[:, None, :] / CUBE
    query_grad = query_grad.astype(jnp.bfloat16).reshape(TOKENS, HD)
    key_picked = jnp.einsum("ctk,ctd->ckd", fine_ds.astype(jnp.float32), query_blocks)
    value_picked = jnp.einsum("ctk,ctd->ckd", fine_half.astype(jnp.float32), grad_blocks)
    key_picked = key_picked.reshape(N_CTX, CUBES_DEV, TOPK, CUBE, HD)
    value_picked = value_picked.reshape(N_CTX, CUBES_DEV, TOPK, CUBE, HD)
    chosen_groups = chosen_rows.reshape(N_CTX, CUBES_DEV, TOPK)
    key_terms = jax.vmap(group_sum)(key_picked, coarse_ds.reshape(N_CTX, CUBES_DEV, NC),
                                    q_cube.reshape(N_CTX, CUBES_DEV, HD), chosen_groups)
    value_terms = jax.vmap(group_sum)(value_picked, coarse_half.reshape(N_CTX, CUBES_DEV, NC),
                                      grad_cube.reshape(N_CTX, CUBES_DEV, HD), chosen_groups)
    key_grad = jnp.sum(key_terms, axis=0).astype(jnp.bfloat16).reshape(TOKENS, HD)
    value_grad = jnp.sum(value_terms, axis=0).astype(jnp.bfloat16).reshape(TOKENS, HD)
    return attention, query_grad, key_grad, value_grad


def heads_first(tensor):
    return tensor.reshape(CLIPS, TOKENS, HEADS, HD).transpose(0, 2, 1, 3).reshape(CLIPS * HEADS, TOKENS, HD)


def heads_back(tensor):
    return tensor.reshape(CLIPS, HEADS, TOKENS, HD).transpose(0, 2, 1, 3).reshape(CLIPS, TOKENS, HEADS * HD)


def reference(queries, key_states, value_states, layer_grad, out_weight, chosen):
    grads_list = []
    for clip_index in range(CLIPS):
        grads_list.append(jnp.dot(layer_grad[clip_index], out_weight.T, preferred_element_type=jnp.float32))
    attn_grad = jnp.stack(grads_list).astype(jnp.bfloat16)
    chosen_heads = jnp.repeat(chosen, HEADS, axis=0)
    results = lax.map(one_head, (heads_first(queries), heads_first(key_states), heads_first(value_states),
                                 heads_first(attn_grad), chosen_heads))
    attention = heads_back(results[0])
    query_grad = heads_back(results[1])
    key_grad = heads_back(results[2])
    value_grad = heads_back(results[3])
    attn_groups = attention.reshape(CLIPS, N_CTX, CUBES_DEV * CUBE, HEADS * HD)
    layer_groups = layer_grad.reshape(CLIPS, N_CTX, CUBES_DEV * CUBE, D)

    def group_weight(running, group_index):
        clip_sum = jnp.zeros((HEADS * HD, D), jnp.float32)
        for clip_index in range(CLIPS):
            term = jnp.dot(attn_groups[clip_index, group_index].T, layer_groups[clip_index, group_index],
                           preferred_element_type=jnp.float32)
            clip_sum = clip_sum + lax.optimization_barrier(term.astype(jnp.bfloat16)).astype(jnp.float32)
        rounded = lax.optimization_barrier(clip_sum.astype(jnp.bfloat16)).astype(jnp.float32)
        return running + rounded, None

    weight_sum, _ = lax.scan(group_weight, jnp.zeros((HEADS * HD, D), jnp.float32),
                             jnp.arange(N_CTX, dtype=jnp.int32))
    return attention, query_grad, key_grad, value_grad, weight_sum.astype(jnp.bfloat16)
```

```python
import jax
import jax.numpy as jnp
from jax import lax
from jax.sharding import PartitionSpec as P

HD = 128
CUBE = 64


def cube_means(blocks):
    grouped = blocks.astype(jnp.float32).reshape(-1, CUBE, blocks.shape[-1])
    return jnp.mean(grouped, axis=1).astype(jnp.bfloat16)


def by_heads(blocks):
    return blocks.reshape(blocks.shape[0], -1, HD)


def softmax_rows(scores):
    largest = jnp.max(scores, axis=-1, keepdims=True)
    expons = jnp.exp(scores - largest)
    return expons / jnp.sum(expons, axis=-1, keepdims=True)


def on_device(queries, key_states, value_states, layer_grad, out_weight, chosen):
    scaling = HD ** (-0.5)
    query_local = queries[0]
    key_local = key_states[0]
    value_local = value_states[0]
    layer_local = layer_grad[0]
    picked = chosen[0]
    tok_local, width = query_local.shape
    heads_here = width // HD
    cubes_local = tok_local // CUBE
    picks_each = picked.shape[1]
    kv_whole = lax.all_gather(
        jnp.concatenate([key_local, value_local], axis=1), "ctx", axis=0, tiled=True
    )
    key_whole, value_whole = kv_whole[:, :width], kv_whole[:, width:]
    columns = lax.all_to_all(layer_local, "clip", split_axis=1, concat_axis=0, tiled=True)
    grad_parts = lax.dot_general(
        columns, out_weight, (((1,), (1,)), ((), ())), preferred_element_type=jnp.float32
    ).astype(jnp.bfloat16)
    grad_parts = lax.all_to_all(
        grad_parts.reshape(-1, tok_local, width), "clip", split_axis=0, concat_axis=0, tiled=True
    )
    attn_grad = jnp.sum(grad_parts.astype(jnp.float32), axis=0).astype(jnp.bfloat16)
    columns_whole = lax.all_gather(columns, "ctx", axis=0, tiled=True)
    tok_whole = key_whole.shape[0]
    cubes_whole = tok_whole // CUBE
    query_cube = cube_means(query_local)
    key_cube, value_cube = cube_means(key_whole), cube_means(value_whole)
    qcube_heads = by_heads(query_cube)
    kcube_heads = by_heads(key_cube)
    vcube_heads = by_heads(value_cube)
    coarse_scores = (
        jnp.einsum("ahd,bhd->hab", qcube_heads, kcube_heads, preferred_element_type=jnp.float32)
        * scaling
    )
    coarse_p = softmax_rows(coarse_scores)
    coarse_half = coarse_p.astype(jnp.bfloat16)
    coarse_out = jnp.einsum(
        "hab,bhd->ahd", coarse_half, vcube_heads, preferred_element_type=jnp.float32
    )
    key_cubes = key_whole.reshape(cubes_whole, CUBE, width)
    value_cubes = value_whole.reshape(cubes_whole, CUBE, width)
    key_pick = key_cubes[picked].reshape(cubes_local, picks_each * CUBE, heads_here, HD)
    value_pick = value_cubes[picked].reshape(cubes_local, picks_each * CUBE, heads_here, HD)
    query_blocks = query_local.reshape(cubes_local, CUBE, heads_here, HD)
    fine_scores = (
        jnp.einsum("cthd,ckhd->chtk", query_blocks, key_pick, preferred_element_type=jnp.float32)
        * scaling
    )
    fine_p = softmax_rows(fine_scores)
    fine_half = fine_p.astype(jnp.bfloat16)
    fine_out = jnp.einsum(
        "chtk,ckhd->cthd", fine_half, value_pick, preferred_element_type=jnp.float32
    )
    attention = (
        (fine_out + coarse_out[:, None, :, :]).astype(jnp.bfloat16).reshape(tok_local, width)
    )
    attention_whole = lax.all_gather(attention, ("ctx", "clip"), axis=0, tiled=True)
    grad_cube = jnp.sum(
        attn_grad.astype(jnp.float32).reshape(cubes_local, CUBE, width), axis=1
    ).astype(jnp.bfloat16)
    gcube_heads = by_heads(grad_cube)
    coarse_dp = jnp.einsum(
        "ahd,bhd->hab", gcube_heads, vcube_heads, preferred_element_type=jnp.float32
    )
    coarse_delta = jnp.sum(coarse_p * coarse_dp, axis=-1, keepdims=True)
    coarse_ds = (scaling * coarse_p * (coarse_dp - coarse_delta)).astype(jnp.bfloat16)
    coarse_dq = jnp.einsum(
        "hab,bhd->ahd", coarse_ds, kcube_heads, preferred_element_type=jnp.float32
    )
    coarse_dk = jnp.einsum(
        "hab,ahd->bhd", coarse_ds, qcube_heads, preferred_element_type=jnp.float32
    )
    coarse_dv = jnp.einsum(
        "hab,ahd->bhd", coarse_half, gcube_heads, preferred_element_type=jnp.float32
    )
    cube_terms = (
        jnp.concatenate(
            [coarse_dk.reshape(cubes_whole, width), coarse_dv.reshape(cubes_whole, width)], axis=1
        )
        / CUBE
    )
    grad_blocks = attn_grad.reshape(cubes_local, CUBE, heads_here, HD)
    fine_dp = jnp.einsum(
        "cthd,ckhd->chtk", grad_blocks, value_pick, preferred_element_type=jnp.float32
    )
    fine_delta = jnp.sum(fine_p * fine_dp, axis=-1, keepdims=True)
    fine_ds = (scaling * fine_p * (fine_dp - fine_delta)).astype(jnp.bfloat16)
    query_grad = jnp.einsum(
        "chtk,ckhd->cthd", fine_ds, key_pick, preferred_element_type=jnp.float32
    )
    query_grad = (query_grad + coarse_dq[:, None, :, :] / CUBE).astype(jnp.bfloat16)
    query_grad = query_grad.reshape(tok_local, width)
    key_picked = jnp.einsum(
        "chtk,cthd->ckhd", fine_ds, query_blocks, preferred_element_type=jnp.float32
    )
    value_picked = jnp.einsum(
        "chtk,cthd->ckhd", fine_half, grad_blocks, preferred_element_type=jnp.float32
    )
    flat_terms = jnp.concatenate(
        [
            key_picked.reshape(cubes_local, picks_each, CUBE, width),
            value_picked.reshape(cubes_local, picks_each, CUBE, width),
        ],
        axis=3,
    )
    flat_terms = flat_terms.reshape(cubes_local * picks_each, CUBE, 2 * width)
    picked_flat = picked.reshape(-1)
    running = jnp.broadcast_to(cube_terms[:, None, :], (cubes_whole, CUBE, 2 * width))
    running = running.at[picked_flat].add(flat_terms)
    summed = lax.psum_scatter(
        running.reshape(tok_whole, 2 * width).astype(jnp.bfloat16),
        "ctx",
        scatter_dimension=0,
        tiled=True,
    ).astype(jnp.float32)
    key_grad = summed[:, :width].astype(jnp.bfloat16)
    value_grad = summed[:, width:].astype(jnp.bfloat16)
    weight_grad = lax.dot_general(
        attention_whole, columns_whole, (((0,), (0,)), ((), ())), preferred_element_type=jnp.float32
    ).astype(jnp.bfloat16)
    return (attention[None], query_grad[None], key_grad[None], value_grad[None], weight_grad)


def solution(mesh):
    placed = (
        P("clip", "ctx", "head"),
        P("clip", "ctx", "head"),
        P("clip", "ctx", "head"),
        P("clip", "ctx", None),
        P("head", "clip"),
        P("clip", "ctx", None),
    )
    return jax.shard_map(
        on_device,
        mesh=mesh,
        in_specs=placed,
        out_specs=(
            P("clip", "ctx", "head"),
            P("clip", "ctx", "head"),
            P("clip", "ctx", "head"),
            P("clip", "ctx", "head"),
            P("head", "clip"),
        ),
        check_vma=False,
    )
```

```python
import functools

import jax
import jax.numpy as jnp
from jax import lax
from jax.experimental import pallas as pl
from jax.experimental.pallas import tpu as pltpu
from jax.sharding import PartitionSpec as P

HD = 128
CUBE = 64


def cube_means(blocks):
    grouped = blocks.astype(jnp.float32).reshape(-1, CUBE, blocks.shape[-1])
    return jnp.mean(grouped, axis=1).astype(jnp.bfloat16)


def by_heads(blocks):
    return blocks.reshape(blocks.shape[0], -1, HD)


def softmax_rows(scores):
    largest = jnp.max(scores, axis=-1, keepdims=True)
    expons = jnp.exp(scores - largest)
    return expons / jnp.sum(expons, axis=-1, keepdims=True)


def on_device(queries, key_states, value_states, layer_grad, out_weight, chosen):
    scaling = HD ** (-0.5)
    query_local = queries[0]
    key_local = key_states[0]
    value_local = value_states[0]
    layer_local = layer_grad[0]
    picked = chosen[0]
    tok_local, width = query_local.shape
    heads_here = width // HD
    cubes_local = tok_local // CUBE
    picks_each = picked.shape[1]
    kv_whole = lax.all_gather(
        jnp.concatenate([key_local, value_local], axis=1), "ctx", axis=0, tiled=True
    )
    key_whole, value_whole = kv_whole[:, :width], kv_whole[:, width:]
    columns = lax.all_to_all(layer_local, "clip", split_axis=1, concat_axis=0, tiled=True)
    grad_parts = lax.dot_general(
        columns, out_weight, (((1,), (1,)), ((), ())), preferred_element_type=jnp.float32
    ).astype(jnp.bfloat16)
    grad_parts = lax.all_to_all(
        grad_parts.reshape(-1, tok_local, width), "clip", split_axis=0, concat_axis=0, tiled=True
    )
    attn_grad = jnp.sum(grad_parts.astype(jnp.float32), axis=0).astype(jnp.bfloat16)
    columns_whole = lax.all_gather(columns, "ctx", axis=0, tiled=True)
    tok_whole = key_whole.shape[0]
    cubes_whole = tok_whole // CUBE
    query_cube = cube_means(query_local)
    key_cube, value_cube = cube_means(key_whole), cube_means(value_whole)
    qcube_heads = by_heads(query_cube)
    kcube_heads = by_heads(key_cube)
    vcube_heads = by_heads(value_cube)
    coarse_scores = (
        jnp.einsum("ahd,bhd->hab", qcube_heads, kcube_heads, preferred_element_type=jnp.float32)
        * scaling
    )
    coarse_p = softmax_rows(coarse_scores)
    coarse_half = coarse_p.astype(jnp.bfloat16)
    coarse_out = jnp.einsum(
        "hab,bhd->ahd", coarse_half, vcube_heads, preferred_element_type=jnp.float32
    )
    key_cubes = key_whole.reshape(cubes_whole, CUBE, width)
    value_cubes = value_whole.reshape(cubes_whole, CUBE, width)
    key_pick = key_cubes[picked].reshape(cubes_local, picks_each * CUBE, heads_here, HD)
    value_pick = value_cubes[picked].reshape(cubes_local, picks_each * CUBE, heads_here, HD)
    query_blocks = query_local.reshape(cubes_local, CUBE, heads_here, HD)
    fine_scores = (
        jnp.einsum("cthd,ckhd->chtk", query_blocks, key_pick, preferred_element_type=jnp.float32)
        * scaling
    )
    fine_p = softmax_rows(fine_scores)
    fine_half = fine_p.astype(jnp.bfloat16)
    fine_out = jnp.einsum(
        "chtk,ckhd->cthd", fine_half, value_pick, preferred_element_type=jnp.float32
    )
    attention = (
        (fine_out + coarse_out[:, None, :, :]).astype(jnp.bfloat16).reshape(tok_local, width)
    )
    attention_whole = lax.all_gather(attention, ("ctx", "clip"), axis=0, tiled=True)
    grad_cube = jnp.sum(
        attn_grad.astype(jnp.float32).reshape(cubes_local, CUBE, width), axis=1
    ).astype(jnp.bfloat16)
    gcube_heads = by_heads(grad_cube)
    coarse_dp = jnp.einsum(
        "ahd,bhd->hab", gcube_heads, vcube_heads, preferred_element_type=jnp.float32
    )
    coarse_delta = jnp.sum(coarse_p * coarse_dp, axis=-1, keepdims=True)
    coarse_ds = (scaling * coarse_p * (coarse_dp - coarse_delta)).astype(jnp.bfloat16)
    coarse_dq = jnp.einsum(
        "hab,bhd->ahd", coarse_ds, kcube_heads, preferred_element_type=jnp.float32
    )
    coarse_dk = jnp.einsum(
        "hab,ahd->bhd", coarse_ds, qcube_heads, preferred_element_type=jnp.float32
    )
    coarse_dv = jnp.einsum(
        "hab,ahd->bhd", coarse_half, gcube_heads, preferred_element_type=jnp.float32
    )
    cube_terms = (
        jnp.concatenate(
            [coarse_dk.reshape(cubes_whole, width), coarse_dv.reshape(cubes_whole, width)], axis=1
        )
        / CUBE
    )
    grad_blocks = attn_grad.reshape(cubes_local, CUBE, heads_here, HD)
    fine_dp = jnp.einsum(
        "cthd,ckhd->chtk", grad_blocks, value_pick, preferred_element_type=jnp.float32
    )
    fine_delta = jnp.sum(fine_p * fine_dp, axis=-1, keepdims=True)
    fine_ds = (scaling * fine_p * (fine_dp - fine_delta)).astype(jnp.bfloat16)
    query_grad = jnp.einsum(
        "chtk,ckhd->cthd", fine_ds, key_pick, preferred_element_type=jnp.float32
    )
    query_grad = (query_grad + coarse_dq[:, None, :, :] / CUBE).astype(jnp.bfloat16)
    query_grad = query_grad.reshape(tok_local, width)
    key_picked = jnp.einsum(
        "chtk,cthd->ckhd", fine_ds, query_blocks, preferred_element_type=jnp.float32
    )
    value_picked = jnp.einsum(
        "chtk,cthd->ckhd", fine_half, grad_blocks, preferred_element_type=jnp.float32
    )
    flat_terms = jnp.concatenate(
        [
            key_picked.reshape(cubes_local, picks_each, CUBE, width),
            value_picked.reshape(cubes_local, picks_each, CUBE, width),
        ],
        axis=3,
    )
    flat_terms = flat_terms.reshape(cubes_local * picks_each, CUBE, 2 * width)
    picked_flat = picked.reshape(-1)
    running = jnp.broadcast_to(cube_terms[:, None, :], (cubes_whole, CUBE, 2 * width))
    running = running.at[picked_flat].add(flat_terms)
    summed = lax.psum_scatter(
        running.reshape(tok_whole, 2 * width).astype(jnp.bfloat16),
        "ctx",
        scatter_dimension=0,
        tiled=True,
    ).astype(jnp.float32)
    key_grad = summed[:, :width].astype(jnp.bfloat16)
    value_grad = summed[:, width:].astype(jnp.bfloat16)
    weight_grad = lax.dot_general(
        attention_whole, columns_whole, (((0,), (0,)), ((), ())), preferred_element_type=jnp.float32
    ).astype(jnp.bfloat16)
    return (attention[None], query_grad[None], key_grad[None], value_grad[None], weight_grad)

ROWS = 16
LOW = -1e30


def dot_nt(a, b):
    return lax.dot_general(a, b, (((1,), (1,)), ((), ())), preferred_element_type=jnp.float32)


def dot_nn(a, b):
    return lax.dot_general(a, b, (((1,), (0,)), ((), ())), preferred_element_type=jnp.float32)


def dot_tn(a, b):
    return lax.dot_general(a, b, (((0,), (0,)), ((), ())), preferred_element_type=jnp.float32)


def cube_rows(blocks, factor):
    at_row = lax.broadcasted_iota(jnp.int32, (ROWS, blocks.shape[1]), 0)
    rows = jnp.zeros((ROWS, blocks.shape[1]), jnp.float32)
    for cube in range(blocks.shape[0] // CUBE):
        part = blocks[cube * CUBE : (cube + 1) * CUBE].astype(jnp.float32)
        total = jnp.sum(part, axis=0, keepdims=True) * factor
        rows = jnp.where(at_row == cube, total, rows)
    return rows.astype(jnp.bfloat16)


def over_tokens(rows, cubes):
    return jnp.concatenate(
        [jnp.broadcast_to(rows[cube : cube + 1], (CUBE, rows.shape[1])) for cube in range(cubes)],
        axis=0,
    )


def pair_kernel(
    n_clip, n_head, chosen, query, key, value, layer, weight,
    attention, query_grad, key_grad, value_grad, weight_grad,
    keys, values, columns, held_weight, fine, coarse, turned,
    partial, partial_in, grad, terms, terms_in,
    kv_sem, deal_sem, share_sem, across_sem, share_far_sem, part_sem, turn_sem, turn_far_sem,
    term_sem, local_sem,
):
    scaling = HD ** (-0.5)
    tokens, width = query.shape
    cols = weight.shape[1]
    heads = width // HD
    cubes = tokens // CUBE
    cubes_whole = 2 * cubes
    quarter = tokens // n_head
    x, h, z = lax.axis_index("ctx"), lax.axis_index("head"), lax.axis_index("clip")
    other = 1 - x
    my_rows = pl.ds(pl.multiple_of(h * quarter, quarter), quarter)

    def to_clip(step):
        return {"clip": lax.rem(z + step, n_clip)}

    def from_clip(step):
        return lax.rem(z + n_clip - step, n_clip)

    def to_head(step):
        return {"head": lax.rem(h + step, n_head)}

    def column_block(clip):
        return pl.ds(pl.multiple_of(clip * cols, cols), cols)

    def slot(ctx, clip):
        return pl.ds(pl.multiple_of((ctx * n_clip + clip) * tokens, tokens), tokens)

    sent = []

    def send(src, dst, sems, index, device):
        copy = pltpu.make_async_remote_copy(
            src_ref=src, dst_ref=dst,
            send_sem=sems.at[(0,) + index], recv_sem=sems.at[(1,) + index],
            device_id=device, device_id_type=pl.DeviceIdType.MESH,
        )
        copy.start()
        sent.append(copy)
        return copy

    weight_copy = pltpu.make_async_copy(weight, held_weight, local_sem.at[0])
    weight_copy.start()
    layer_copy = pltpu.make_async_copy(
        layer.at[:, column_block(z)], columns.at[x, z], local_sem.at[1]
    )
    layer_copy.start()

    barrier = pltpu.get_barrier_semaphore()
    partners = [{"ctx": other}]
    partners += [to_clip(step) for step in range(1, n_clip)]
    partners += [to_head(step) for step in range(1, n_head)]
    for partner in partners:
        pl.semaphore_signal(barrier, inc=1, device_id=partner, device_id_type=pl.DeviceIdType.MESH)
    pl.semaphore_wait(barrier, len(partners))

    mine = pl.ds(pl.multiple_of(x * tokens, tokens), tokens)
    key_copy = send(key, keys.at[mine], kv_sem, (0,), {"ctx": other})
    value_copy = send(value, values.at[mine], kv_sem, (1,), {"ctx": other})
    deals = [None]
    for step in range(1, n_clip):
        deals.append(
            send(
                layer.at[my_rows, column_block(lax.rem(z + step, n_clip))],
                columns.at[x, z, my_rows], deal_sem, (step,), to_clip(step),
            )
        )
    across = [
        send(
            layer.at[my_rows, column_block(z)], columns.at[x, z, my_rows],
            across_sem, (0,), {"ctx": other},
        )
    ]
    keys[mine, :] = key[...]
    values[mine, :] = value[...]
    query_cube = cube_rows(query[...], 1.0 / CUBE)
    column_cube = lax.broadcasted_iota(jnp.int32, (1, cubes_whole * CUBE), 1) // CUBE
    allowed = []
    for cube in range(cubes):
        hit = column_cube == chosen[cube, 0]
        for pick in range(1, chosen.shape[1]):
            hit = hit | (column_cube == chosen[cube, pick])
        allowed.append(jnp.broadcast_to(hit.astype(jnp.float32), (CUBE, cubes_whole * CUBE)))
    allowed = jnp.concatenate(allowed, axis=0) > 0.5
    real = lax.broadcasted_iota(jnp.int32, (ROWS, ROWS), 1) < cubes_whole

    shares = [None]

    def pass_on(step):
        deals[step].wait_recv()
        piece = columns.at[x, from_clip(step), my_rows]
        shares.append(
            [send(piece, piece, share_sem, (step, turn), to_head(turn)) for turn in range(1, n_head)]
        )
        across.append(send(piece, piece, across_sem, (step,), {"ctx": other}))

    key_copy.wait_recv()
    value_copy.wait_recv()
    key_cube = cube_rows(keys[...], 1.0 / CUBE)
    value_cube = cube_rows(values[...], 1.0 / CUBE)
    for step in range(1, n_clip):
        pass_on(step)

    for head in range(heads):
        at = slice(head * HD, (head + 1) * HD)
        scores = dot_nt(query[:, at], keys[:, at]) * scaling
        scores = jnp.where(allowed, scores, LOW)
        expons = jnp.exp(scores - jnp.max(scores, axis=-1, keepdims=True))
        fine_p = expons / jnp.sum(expons, axis=-1, keepdims=True)
        fine[head] = fine_p
        coarse_scores = dot_nt(query_cube[:, at], key_cube[:, at]) * scaling
        coarse_scores = jnp.where(real, coarse_scores, LOW)
        expons = jnp.exp(coarse_scores - jnp.max(coarse_scores, axis=-1, keepdims=True))
        coarse_p = expons / jnp.sum(expons, axis=-1, keepdims=True)
        coarse[head] = coarse_p
        coarse_out = dot_nn(coarse_p.astype(jnp.bfloat16), value_cube[:, at])
        fine_out = dot_nn(fine_p.astype(jnp.bfloat16), values[:, at])
        result = (fine_out + over_tokens(coarse_out, cubes)).astype(jnp.bfloat16)
        attention[:, at] = result
        turned[at, slot(x, z)] = result.astype(jnp.float32).T.astype(jnp.bfloat16)

    own_slot = turned.at[:, slot(x, z)]
    turn_far = [send(own_slot, own_slot, turn_far_sem, (0,), {"ctx": other})]

    weight_copy.wait()
    layer_copy.wait()
    parts = [None]
    for step in range(1, n_clip):
        clip = from_clip(step)
        for copy in shares[step]:
            copy.wait_recv()
        partial[step] = dot_nt(columns[x, clip], held_weight[...]).astype(jnp.bfloat16)
        parts.append(
            send(
                partial.at[step], partial_in.at[step], part_sem, (step,),
                {"clip": clip},
            )
        )
    turns = [None]
    for step in range(1, n_clip):
        turns.append(send(own_slot, own_slot, turn_sem, (step,), to_clip(step)))
    total = dot_nt(columns[x, z], held_weight[...])
    for copy in across:
        copy.wait_recv()
    far = columns.at[other, :, my_rows]
    share_far = [
        send(far, far, share_far_sem, (turn,), to_head(turn)) for turn in range(1, n_head)
    ]
    for step in range(1, n_clip):
        parts[step].wait_recv()
        total = total + partial_in[step].astype(jnp.float32)
    grad[...] = total.astype(jnp.bfloat16)
    grad_cube = cube_rows(grad[...], 1.0)

    for head in range(heads):
        at = slice(head * HD, (head + 1) * HD)
        after = slice(width + head * HD, width + (head + 1) * HD)
        fine_p = fine[head]
        fine_half = fine_p.astype(jnp.bfloat16)
        fine_dp = dot_nt(grad[:, at], values[:, at])
        delta = jnp.sum(fine_p * fine_dp, axis=-1, keepdims=True)
        fine_ds = (scaling * fine_p * (fine_dp - delta)).astype(jnp.bfloat16)
        coarse_p = coarse[head]
        coarse_half = coarse_p.astype(jnp.bfloat16)
        coarse_dp = dot_nt(grad_cube[:, at], value_cube[:, at])
        delta = jnp.sum(coarse_p * coarse_dp, axis=-1, keepdims=True)
        coarse_ds = (scaling * coarse_p * (coarse_dp - delta)).astype(jnp.bfloat16)
        coarse_dq = dot_nn(coarse_ds, key_cube[:, at]) * (1.0 / CUBE)
        coarse_dk = dot_tn(coarse_ds, query_cube[:, at]) * (1.0 / CUBE)
        coarse_dv = dot_tn(coarse_half, grad_cube[:, at]) * (1.0 / CUBE)
        dq = dot_nn(fine_ds, keys[:, at]) + over_tokens(coarse_dq, cubes)
        query_grad[:, at] = dq.astype(jnp.bfloat16)
        dk = dot_tn(fine_ds, query[:, at]) + over_tokens(coarse_dk, cubes_whole)
        dv = dot_tn(fine_half, grad[:, at]) + over_tokens(coarse_dv, cubes_whole)
        dk, dv = dk.astype(jnp.bfloat16), dv.astype(jnp.bfloat16)
        for ctx in range(2):
            terms[ctx, :, at] = dk[ctx * tokens : (ctx + 1) * tokens]
            terms[ctx, :, after] = dv[ctx * tokens : (ctx + 1) * tokens]

    term_copy = send(terms.at[other], terms_in, term_sem, (), {"ctx": other})

    for step in range(1, n_clip):
        turns[step].wait_recv()
        arrived = turned.at[:, slot(x, from_clip(step))]
        turn_far.append(send(arrived, arrived, turn_far_sem, (step,), {"ctx": other}))
    for copy in share_far + turn_far:
        copy.wait_recv()
    tile = 256
    for begin in range(0, cols, tile):
        block = columns[:, :, :, begin : begin + tile].reshape(2 * n_clip * tokens, tile)
        weight_grad[:, begin : begin + tile] = dot_nn(turned[...], block).astype(jnp.bfloat16)

    term_copy.wait_recv()
    summed = terms[x].astype(jnp.float32) + terms_in[...].astype(jnp.float32)
    key_grad[...] = summed[:, :width].astype(jnp.bfloat16)
    value_grad[...] = summed[:, width:].astype(jnp.bfloat16)
    for copy in sent:
        copy.wait_send()


def paired(n_clip, n_head, queries, key_states, value_states, layer_grad, out_weight, chosen):
    tokens, width = queries.shape[1:]
    cols = out_weight.shape[1]
    heads = width // HD
    half = jnp.bfloat16
    whole = 2 * tokens
    vmem = pl.BlockSpec(memory_space=pltpu.VMEM)
    anywhere = pl.BlockSpec(memory_space=pl.ANY)
    small = jax.ShapeDtypeStruct((tokens, width), half)
    dma = pltpu.SemaphoreType.DMA
    outs = pl.pallas_call(
        functools.partial(pair_kernel, n_clip, n_head),
        out_shape=(small, small, small, small, jax.ShapeDtypeStruct((width, cols), half)),
        in_specs=[pl.BlockSpec(memory_space=pltpu.SMEM), vmem, vmem, vmem, anywhere, anywhere],
        out_specs=(vmem,) * 5,
        scratch_shapes=[
            pltpu.VMEM((whole, width), half),
            pltpu.VMEM((whole, width), half),
            pltpu.VMEM((2, n_clip, tokens, cols), half),
            pltpu.VMEM((width, cols), half),
            pltpu.VMEM((heads, tokens, whole), jnp.float32),
            pltpu.VMEM((heads, ROWS, ROWS), jnp.float32),
            pltpu.VMEM((width, 2 * n_clip * tokens), half),
            pltpu.VMEM((n_clip, tokens, width), half),
            pltpu.VMEM((n_clip, tokens, width), half),
            pltpu.VMEM((tokens, width), half),
            pltpu.VMEM((2, tokens, 2 * width), half),
            pltpu.VMEM((tokens, 2 * width), half),
            dma((2, 2)),
            dma((2, n_clip)),
            dma((2, n_clip, n_head)),
            dma((2, n_clip)),
            dma((2, n_head)),
            dma((2, n_clip)),
            dma((2, n_clip)),
            dma((2, n_clip)),
            dma((2,)),
            dma((2,)),
        ],
        compiler_params=pltpu.CompilerParams(
            collective_id=0, has_side_effects=True, vmem_limit_bytes=40 * 2**20
        ),
    )(chosen[0], queries[0], key_states[0], value_states[0], layer_grad[0], out_weight)
    return tuple(out[None] for out in outs[:4]) + (outs[4],)


def solution(mesh):
    clips, heads = mesh.shape["clip"], mesh.shape["head"]
    paired_here = mesh.shape["ctx"] == 2
    body = functools.partial(paired, clips, heads) if paired_here else on_device
    placed = (
        P("clip", "ctx", "head"),
        P("clip", "ctx", "head"),
        P("clip", "ctx", "head"),
        P("clip", "ctx", None),
        P("head", "clip"),
        P("clip", "ctx", None),
    )
    return jax.shard_map(
        body,
        mesh=mesh,
        in_specs=placed,
        out_specs=(
            P("clip", "ctx", "head"),
            P("clip", "ctx", "head"),
            P("clip", "ctx", "head"),
            P("clip", "ctx", "head"),
            P("head", "clip"),
        ),
        check_vma=False,
    )
```

```python
import functools

import jax
import jax.numpy as jnp
from jax import lax
from jax.experimental import pallas as pl
from jax.experimental.pallas import tpu as pltpu
from jax.sharding import PartitionSpec as P

HD = 128
CUBE = 64


def cube_means(blocks):
    grouped = blocks.astype(jnp.float32).reshape(-1, CUBE, blocks.shape[-1])
    return jnp.mean(grouped, axis=1).astype(jnp.bfloat16)


def by_heads(blocks):
    return blocks.reshape(blocks.shape[0], -1, HD)


def softmax_rows(scores):
    largest = jnp.max(scores, axis=-1, keepdims=True)
    expons = jnp.exp(scores - largest)
    return expons / jnp.sum(expons, axis=-1, keepdims=True)


def on_device(queries, key_states, value_states, layer_grad, out_weight, chosen):
    scaling = HD ** (-0.5)
    query_local = queries[0]
    key_local = key_states[0]
    value_local = value_states[0]
    layer_local = layer_grad[0]
    picked = chosen[0]
    tok_local, width = query_local.shape
    heads_here = width // HD
    cubes_local = tok_local // CUBE
    picks_each = picked.shape[1]
    kv_whole = lax.all_gather(
        jnp.concatenate([key_local, value_local], axis=1), "ctx", axis=0, tiled=True
    )
    key_whole, value_whole = kv_whole[:, :width], kv_whole[:, width:]
    columns = lax.all_to_all(layer_local, "clip", split_axis=1, concat_axis=0, tiled=True)
    grad_parts = lax.dot_general(
        columns, out_weight, (((1,), (1,)), ((), ())), preferred_element_type=jnp.float32
    ).astype(jnp.bfloat16)
    grad_parts = lax.all_to_all(
        grad_parts.reshape(-1, tok_local, width), "clip", split_axis=0, concat_axis=0, tiled=True
    )
    attn_grad = jnp.sum(grad_parts.astype(jnp.float32), axis=0).astype(jnp.bfloat16)
    columns_whole = lax.all_gather(columns, "ctx", axis=0, tiled=True)
    tok_whole = key_whole.shape[0]
    cubes_whole = tok_whole // CUBE
    query_cube = cube_means(query_local)
    key_cube, value_cube = cube_means(key_whole), cube_means(value_whole)
    qcube_heads = by_heads(query_cube)
    kcube_heads = by_heads(key_cube)
    vcube_heads = by_heads(value_cube)
    coarse_scores = (
        jnp.einsum("ahd,bhd->hab", qcube_heads, kcube_heads, preferred_element_type=jnp.float32)
        * scaling
    )
    coarse_p = softmax_rows(coarse_scores)
    coarse_half = coarse_p.astype(jnp.bfloat16)
    coarse_out = jnp.einsum(
        "hab,bhd->ahd", coarse_half, vcube_heads, preferred_element_type=jnp.float32
    )
    key_cubes = key_whole.reshape(cubes_whole, CUBE, width)
    value_cubes = value_whole.reshape(cubes_whole, CUBE, width)
    key_pick = key_cubes[picked].reshape(cubes_local, picks_each * CUBE, heads_here, HD)
    value_pick = value_cubes[picked].reshape(cubes_local, picks_each * CUBE, heads_here, HD)
    query_blocks = query_local.reshape(cubes_local, CUBE, heads_here, HD)
    fine_scores = (
        jnp.einsum("cthd,ckhd->chtk", query_blocks, key_pick, preferred_element_type=jnp.float32)
        * scaling
    )
    fine_p = softmax_rows(fine_scores)
    fine_half = fine_p.astype(jnp.bfloat16)
    fine_out = jnp.einsum(
        "chtk,ckhd->cthd", fine_half, value_pick, preferred_element_type=jnp.float32
    )
    attention = (
        (fine_out + coarse_out[:, None, :, :]).astype(jnp.bfloat16).reshape(tok_local, width)
    )
    attention_whole = lax.all_gather(attention, ("ctx", "clip"), axis=0, tiled=True)
    grad_cube = jnp.sum(
        attn_grad.astype(jnp.float32).reshape(cubes_local, CUBE, width), axis=1
    ).astype(jnp.bfloat16)
    gcube_heads = by_heads(grad_cube)
    coarse_dp = jnp.einsum(
        "ahd,bhd->hab", gcube_heads, vcube_heads, preferred_element_type=jnp.float32
    )
    coarse_delta = jnp.sum(coarse_p * coarse_dp, axis=-1, keepdims=True)
    coarse_ds = (scaling * coarse_p * (coarse_dp - coarse_delta)).astype(jnp.bfloat16)
    coarse_dq = jnp.einsum(
        "hab,bhd->ahd", coarse_ds, kcube_heads, preferred_element_type=jnp.float32
    )
    coarse_dk = jnp.einsum(
        "hab,ahd->bhd", coarse_ds, qcube_heads, preferred_element_type=jnp.float32
    )
    coarse_dv = jnp.einsum(
        "hab,ahd->bhd", coarse_half, gcube_heads, preferred_element_type=jnp.float32
    )
    cube_terms = (
        jnp.concatenate(
            [coarse_dk.reshape(cubes_whole, width), coarse_dv.reshape(cubes_whole, width)], axis=1
        )
        / CUBE
    )
    grad_blocks = attn_grad.reshape(cubes_local, CUBE, heads_here, HD)
    fine_dp = jnp.einsum(
        "cthd,ckhd->chtk", grad_blocks, value_pick, preferred_element_type=jnp.float32
    )
    fine_delta = jnp.sum(fine_p * fine_dp, axis=-1, keepdims=True)
    fine_ds = (scaling * fine_p * (fine_dp - fine_delta)).astype(jnp.bfloat16)
    query_grad = jnp.einsum(
        "chtk,ckhd->cthd", fine_ds, key_pick, preferred_element_type=jnp.float32
    )
    query_grad = (query_grad + coarse_dq[:, None, :, :] / CUBE).astype(jnp.bfloat16)
    query_grad = query_grad.reshape(tok_local, width)
    key_picked = jnp.einsum(
        "chtk,cthd->ckhd", fine_ds, query_blocks, preferred_element_type=jnp.float32
    )
    value_picked = jnp.einsum(
        "chtk,cthd->ckhd", fine_half, grad_blocks, preferred_element_type=jnp.float32
    )
    flat_terms = jnp.concatenate(
        [
            key_picked.reshape(cubes_local, picks_each, CUBE, width),
            value_picked.reshape(cubes_local, picks_each, CUBE, width),
        ],
        axis=3,
    )
    flat_terms = flat_terms.reshape(cubes_local * picks_each, CUBE, 2 * width)
    picked_flat = picked.reshape(-1)
    running = jnp.broadcast_to(cube_terms[:, None, :], (cubes_whole, CUBE, 2 * width))
    running = running.at[picked_flat].add(flat_terms)
    summed = lax.psum_scatter(
        running.reshape(tok_whole, 2 * width).astype(jnp.bfloat16),
        "ctx",
        scatter_dimension=0,
        tiled=True,
    ).astype(jnp.float32)
    key_grad = summed[:, :width].astype(jnp.bfloat16)
    value_grad = summed[:, width:].astype(jnp.bfloat16)
    weight_grad = lax.dot_general(
        attention_whole, columns_whole, (((0,), (0,)), ((), ())), preferred_element_type=jnp.float32
    ).astype(jnp.bfloat16)
    return (attention[None], query_grad[None], key_grad[None], value_grad[None], weight_grad)

ROWS = 16
LOW = -1e30


def dot_nt(a, b):
    return lax.dot_general(a, b, (((1,), (1,)), ((), ())), preferred_element_type=jnp.float32)


def dot_nn(a, b):
    return lax.dot_general(a, b, (((1,), (0,)), ((), ())), preferred_element_type=jnp.float32)


def dot_tn(a, b):
    return lax.dot_general(a, b, (((0,), (0,)), ((), ())), preferred_element_type=jnp.float32)


def cube_rows(blocks, factor):
    at_row = lax.broadcasted_iota(jnp.int32, (ROWS, blocks.shape[1]), 0)
    rows = jnp.zeros((ROWS, blocks.shape[1]), jnp.float32)
    for cube in range(blocks.shape[0] // CUBE):
        part = blocks[cube * CUBE : (cube + 1) * CUBE].astype(jnp.float32)
        total = jnp.sum(part, axis=0, keepdims=True) * factor
        rows = jnp.where(at_row == cube, total, rows)
    return rows.astype(jnp.bfloat16)


def over_tokens(rows, cubes):
    return jnp.concatenate(
        [jnp.broadcast_to(rows[cube : cube + 1], (CUBE, rows.shape[1])) for cube in range(cubes)],
        axis=0,
    )


def pair_kernel(
    n_clip, n_head, chosen_in, query_in, key, value, layer, weight,
    attention_out, query_grad_out, key_grad_out, value_grad_out, weight_grad_out,
    attention, query_grad, key_grad, value_grad, weight_grad, chosen, query, keys, values, columns, held_weight, weight_t, fine, coarse, turned,
    partial, partial_in, grad, terms, terms_in,
    kv_sem, deal_sem, share_sem, across_sem, share_far_sem, part_sem, turn_sem, turn_far_sem,
    term_sem, local_sem, out_sem,
):
    scaling = HD ** (-0.5)
    tokens, width = query_in.shape
    cols = weight.shape[1]
    heads = width // HD
    cubes = tokens // CUBE
    cubes_whole = 2 * cubes
    quarter = tokens // n_head
    x, h, z = lax.axis_index("ctx"), lax.axis_index("head"), lax.axis_index("clip")
    other = 1 - x
    my_rows = pl.ds(pl.multiple_of(h * quarter, quarter), quarter)

    def to_clip(step):
        return {"clip": lax.rem(z + step, n_clip)}

    def from_clip(step):
        return lax.rem(z + n_clip - step, n_clip)

    def to_head(step):
        return {"head": lax.rem(h + step, n_head)}

    def column_block(clip):
        return pl.ds(pl.multiple_of(clip * cols, cols), cols)

    def slot(ctx, clip):
        return pl.ds(pl.multiple_of((ctx * n_clip + clip) * tokens, tokens), tokens)

    sent, written = [], []

    def write(src, dst):
        copy = pltpu.make_async_copy(src, dst, out_sem.at[len(written)])
        copy.start()
        written.append(copy)

    def send(src, dst, sems, index, device):
        copy = pltpu.make_async_remote_copy(
            src_ref=src, dst_ref=dst,
            send_sem=sems.at[(0,) + index], recv_sem=sems.at[(1,) + index],
            device_id=device, device_id_type=pl.DeviceIdType.MESH,
        )
        copy.start()
        sent.append(copy)
        return copy

    mine = pl.ds(pl.multiple_of(x * tokens, tokens), tokens)
    locals_in = [
        pltpu.make_async_copy(src, dst, local_sem.at[index])
        for index, (src, dst) in enumerate(
            [
                (query_in, query),
                (key, keys.at[mine]),
                (value, values.at[mine]),
                (weight, held_weight),
                (layer.at[:, column_block(z)], columns.at[x, z]),
                (chosen_in, chosen),
            ]
        )
    ]
    for copy in locals_in:
        copy.start()

    barrier = pltpu.get_barrier_semaphore()
    partners = [{"ctx": other}]
    partners += [to_clip(step) for step in range(1, n_clip)]
    partners += [to_head(step) for step in range(1, n_head)]
    for partner in partners:
        pl.semaphore_signal(barrier, inc=1, device_id=partner, device_id_type=pl.DeviceIdType.MESH)
    pl.semaphore_wait(barrier, len(partners))

    key_copy = send(key, keys.at[mine], kv_sem, (0,), {"ctx": other})
    value_copy = send(value, values.at[mine], kv_sem, (1,), {"ctx": other})
    deals = [None]
    for step in range(1, n_clip):
        deals.append(
            send(
                layer.at[my_rows, column_block(lax.rem(z + step, n_clip))],
                columns.at[x, z, my_rows], deal_sem, (step,), to_clip(step),
            )
        )
    across = [
        send(
            layer.at[my_rows, column_block(z)], columns.at[x, z, my_rows],
            across_sem, (0,), {"ctx": other},
        )
    ]
    for copy in locals_in:
        copy.wait()
    for head in range(heads):
        at = slice(head * HD, (head + 1) * HD)
        weight_t[:, at] = held_weight[at, :].T
    query_cube = cube_rows(query[...], 1.0 / CUBE)
    column_cube = lax.broadcasted_iota(jnp.int32, (1, cubes_whole * CUBE), 1) // CUBE
    allowed = []
    for cube in range(cubes):
        hit = column_cube == chosen[cube, 0]
        for pick in range(1, chosen.shape[1]):
            hit = hit | (column_cube == chosen[cube, pick])
        allowed.append(jnp.broadcast_to(hit.astype(jnp.float32), (CUBE, cubes_whole * CUBE)))
    allowed = jnp.concatenate(allowed, axis=0) > 0.5
    real = lax.broadcasted_iota(jnp.int32, (ROWS, ROWS), 1) < cubes_whole

    shares = [None]

    def pass_on(step):
        deals[step].wait_recv()
        piece = columns.at[x, from_clip(step), my_rows]
        shares.append(
            [send(piece, piece, share_sem, (step, turn), to_head(turn)) for turn in range(1, n_head)]
        )
        across.append(send(piece, piece, across_sem, (step,), {"ctx": other}))

    key_copy.wait_recv()
    value_copy.wait_recv()
    key_cube = cube_rows(keys[...], 1.0 / CUBE)
    value_cube = cube_rows(values[...], 1.0 / CUBE)
    for step in range(1, n_clip):
        pass_on(step)

    early = (heads + 1) // 2
    split = (slice(0, early * HD), slice(early * HD, width))
    turns, turn_far = [], []

    def turn_out(part):
        piece = turned.at[split[part], slot(x, z)]
        turns.append(
            [send(piece, piece, turn_sem, (part, step), to_clip(step)) for step in range(1, n_clip)]
        )

    def turn_across(part, step):
        piece = turned.at[split[part], slot(x, from_clip(step))]
        turn_far.append(send(piece, piece, turn_far_sem, (part, step), {"ctx": other}))

    for head in range(heads):
        at = slice(head * HD, (head + 1) * HD)
        scores = dot_nt(query[:, at], keys[:, at]) * scaling
        scores = jnp.where(allowed, scores, LOW)
        expons = jnp.exp(scores - jnp.max(scores, axis=-1, keepdims=True))
        fine_p = expons / jnp.sum(expons, axis=-1, keepdims=True)
        fine[head] = fine_p
        coarse_scores = dot_nt(query_cube[:, at], key_cube[:, at]) * scaling
        coarse_scores = jnp.where(real, coarse_scores, LOW)
        expons = jnp.exp(coarse_scores - jnp.max(coarse_scores, axis=-1, keepdims=True))
        coarse_p = expons / jnp.sum(expons, axis=-1, keepdims=True)
        coarse[head] = coarse_p
        coarse_out = dot_nn(coarse_p.astype(jnp.bfloat16), value_cube[:, at])
        fine_out = dot_nn(fine_p.astype(jnp.bfloat16), values[:, at])
        result = (fine_out + over_tokens(coarse_out, cubes)).astype(jnp.bfloat16)
        attention[:, at] = result
        turned[at, slot(x, z)] = result.astype(jnp.float32).T.astype(jnp.bfloat16)
        if head == early - 1:
            turn_out(0)
            turn_across(0, 0)
    turn_across(1, 0)
    write(attention, attention_out)

    parts = [None]
    for step in range(1, n_clip):
        clip = from_clip(step)
        for copy in shares[step]:
            copy.wait_recv()
        partial[step] = dot_nn(columns[x, clip], weight_t[...]).astype(jnp.bfloat16)
        parts.append(
            send(
                partial.at[step], partial_in.at[step], part_sem, (step,),
                {"clip": clip},
            )
        )
    total = dot_nn(columns[x, z], weight_t[...])
    for copy in across:
        copy.wait_recv()
    far = columns.at[other, :, my_rows]
    share_far = [
        send(far, far, share_far_sem, (turn,), to_head(turn)) for turn in range(1, n_head)
    ]
    for step in range(1, n_clip):
        turns[0][step - 1].wait_recv()
        turn_across(0, step)
    for step in range(1, n_clip):
        parts[step].wait_recv()
        total = total + partial_in[step].astype(jnp.float32)
    turn_out(1)
    grad[...] = total.astype(jnp.bfloat16)
    grad_cube = cube_rows(grad[...], 1.0)

    for head in range(heads):
        at = slice(head * HD, (head + 1) * HD)
        after = slice(width + head * HD, width + (head + 1) * HD)
        fine_p = fine[head]
        fine_half = fine_p.astype(jnp.bfloat16)
        fine_dp = dot_nt(grad[:, at], values[:, at])
        delta = jnp.sum(fine_p * fine_dp, axis=-1, keepdims=True)
        fine_ds = (scaling * fine_p * (fine_dp - delta)).astype(jnp.bfloat16)
        coarse_p = coarse[head]
        coarse_half = coarse_p.astype(jnp.bfloat16)
        coarse_dp = dot_nt(grad_cube[:, at], value_cube[:, at])
        delta = jnp.sum(coarse_p * coarse_dp, axis=-1, keepdims=True)
        coarse_ds = (scaling * coarse_p * (coarse_dp - delta)).astype(jnp.bfloat16)
        coarse_dq = dot_nn(coarse_ds, key_cube[:, at]) * (1.0 / CUBE)
        coarse_dk = dot_tn(coarse_ds, query_cube[:, at]) * (1.0 / CUBE)
        coarse_dv = dot_tn(coarse_half, grad_cube[:, at]) * (1.0 / CUBE)
        dq = dot_nn(fine_ds, keys[:, at]) + over_tokens(coarse_dq, cubes)
        query_grad[:, at] = dq.astype(jnp.bfloat16)
        dk = dot_tn(fine_ds, query[:, at]) + over_tokens(coarse_dk, cubes_whole)
        dv = dot_tn(fine_half, grad[:, at]) + over_tokens(coarse_dv, cubes_whole)
        dk, dv = dk.astype(jnp.bfloat16), dv.astype(jnp.bfloat16)
        for ctx in range(2):
            terms[ctx, :, at] = dk[ctx * tokens : (ctx + 1) * tokens]
            terms[ctx, :, after] = dv[ctx * tokens : (ctx + 1) * tokens]

    write(query_grad, query_grad_out)
    term_copy = send(terms.at[other], terms_in, term_sem, (), {"ctx": other})

    for step in range(1, n_clip):
        turns[1][step - 1].wait_recv()
        turn_across(1, step)
    for copy in share_far + turn_far:
        copy.wait_recv()
    tile = 256
    for begin in range(0, cols, tile):
        block = columns[:, :, :, begin : begin + tile].reshape(2 * n_clip * tokens, tile)
        weight_grad[:, begin : begin + tile] = dot_nn(turned[...], block).astype(jnp.bfloat16)
        tile_at = slice(begin, begin + tile)
        write(weight_grad.at[:, tile_at], weight_grad_out.at[:, tile_at])

    term_copy.wait_recv()
    summed = terms[x].astype(jnp.float32) + terms_in[...].astype(jnp.float32)
    key_grad[...] = summed[:, :width].astype(jnp.bfloat16)
    value_grad[...] = summed[:, width:].astype(jnp.bfloat16)
    write(key_grad, key_grad_out)
    write(value_grad, value_grad_out)
    for copy in sent:
        copy.wait_send()
    for copy in written:
        copy.wait()


def copy_out(*refs):
    sem = refs[-1]
    copies = [
        pltpu.make_async_copy(refs[index], refs[5 + index], sem.at[index]) for index in range(5)
    ]
    for copy in copies:
        copy.start()
    for copy in copies:
        copy.wait()


def paired(n_clip, n_head, queries, key_states, value_states, layer_grad, out_weight, chosen):
    tokens, width = queries.shape[1:]
    cols = out_weight.shape[1]
    heads = width // HD
    half = jnp.bfloat16
    whole = 2 * tokens
    far = pl.BlockSpec(memory_space=pltpu.HBM)
    small = jax.ShapeDtypeStruct((tokens, width), half)
    dma = pltpu.SemaphoreType.DMA
    outs = pl.pallas_call(
        functools.partial(pair_kernel, n_clip, n_head),
        out_shape=(small, small, small, small, jax.ShapeDtypeStruct((width, cols), half)),
        in_specs=[far] * 6,
        out_specs=(far,) * 5,
        scratch_shapes=[pltpu.VMEM((tokens, width), half)] * 4
        + [
            pltpu.VMEM((width, cols), half),
            pltpu.SMEM(chosen.shape[1:], jnp.int32),
            pltpu.VMEM((tokens, width), half),
            pltpu.VMEM((whole, width), half),
            pltpu.VMEM((whole, width), half),
            pltpu.VMEM((2, n_clip, tokens, cols), half),
            pltpu.VMEM((width, cols), half),
            pltpu.VMEM((cols, width), half),
            pltpu.VMEM((heads, tokens, whole), jnp.float32),
            pltpu.VMEM((heads, ROWS, ROWS), jnp.float32),
            pltpu.VMEM((width, 2 * n_clip * tokens), half),
            pltpu.VMEM((n_clip, tokens, width), half),
            pltpu.VMEM((n_clip, tokens, width), half),
            pltpu.VMEM((tokens, width), half),
            pltpu.VMEM((2, tokens, 2 * width), half),
            pltpu.VMEM((tokens, 2 * width), half),
            dma((2, 2)),
            dma((2, n_clip)),
            dma((2, n_clip, n_head)),
            dma((2, n_clip)),
            dma((2, n_head)),
            dma((2, n_clip)),
            dma((2, 2, n_clip)),
            dma((2, 2, n_clip)),
            dma((2,)),
            dma((6,)),
            dma((4 + cols // 256,)),
        ],
        compiler_params=pltpu.CompilerParams(
            collective_id=0, has_side_effects=True, vmem_limit_bytes=60 * 2**20
        ),
    )(chosen[0], queries[0], key_states[0], value_states[0], layer_grad[0], out_weight)
    outs = pl.pallas_call(
        copy_out,
        out_shape=tuple(jax.ShapeDtypeStruct(out.shape, half) for out in outs),
        in_specs=[far] * 5,
        out_specs=(far,) * 5,
        scratch_shapes=[dma((5,))],
        compiler_params=pltpu.CompilerParams(vmem_limit_bytes=60 * 2**20),
    )(*outs)
    return tuple(out[None] for out in outs[:4]) + (outs[4],)


def solution(mesh):
    clips, heads = mesh.shape["clip"], mesh.shape["head"]
    paired_here = mesh.shape["ctx"] == 2
    body = functools.partial(paired, clips, heads) if paired_here else on_device
    placed = (
        P("clip", "ctx", "head"),
        P("clip", "ctx", "head"),
        P("clip", "ctx", "head"),
        P("clip", "ctx", None),
        P("head", "clip"),
        P("clip", "ctx", None),
    )
    return jax.shard_map(
        body,
        mesh=mesh,
        in_specs=placed,
        out_specs=(
            P("clip", "ctx", "head"),
            P("clip", "ctx", "head"),
            P("clip", "ctx", "head"),
            P("clip", "ctx", "head"),
            P("head", "clip"),
        ),
        check_vma=False,
    )
```

```python
import functools

import jax
import jax.numpy as jnp
from jax import lax
from jax.experimental import pallas as pl
from jax.experimental.pallas import tpu as pltpu
from jax.sharding import PartitionSpec as P

HD = 128
CUBE = 64


def cube_means(blocks):
    grouped = blocks.astype(jnp.float32).reshape(-1, CUBE, blocks.shape[-1])
    return jnp.mean(grouped, axis=1).astype(jnp.bfloat16)


def by_heads(blocks):
    return blocks.reshape(blocks.shape[0], -1, HD)


def softmax_rows(scores):
    largest = jnp.max(scores, axis=-1, keepdims=True)
    expons = jnp.exp(scores - largest)
    return expons / jnp.sum(expons, axis=-1, keepdims=True)


def on_device(queries, key_states, value_states, layer_grad, out_weight, chosen):
    scaling = HD ** (-0.5)
    query_local = queries[0]
    key_local = key_states[0]
    value_local = value_states[0]
    layer_local = layer_grad[0]
    picked = chosen[0]
    tok_local, width = query_local.shape
    heads_here = width // HD
    cubes_local = tok_local // CUBE
    picks_each = picked.shape[1]
    kv_whole = lax.all_gather(
        jnp.concatenate([key_local, value_local], axis=1), "ctx", axis=0, tiled=True
    )
    key_whole, value_whole = kv_whole[:, :width], kv_whole[:, width:]
    columns = lax.all_to_all(layer_local, "clip", split_axis=1, concat_axis=0, tiled=True)
    grad_parts = lax.dot_general(
        columns, out_weight, (((1,), (1,)), ((), ())), preferred_element_type=jnp.float32
    ).astype(jnp.bfloat16)
    grad_parts = lax.all_to_all(
        grad_parts.reshape(-1, tok_local, width), "clip", split_axis=0, concat_axis=0, tiled=True
    )
    attn_grad = jnp.sum(grad_parts.astype(jnp.float32), axis=0).astype(jnp.bfloat16)
    columns_whole = lax.all_gather(columns, "ctx", axis=0, tiled=True)
    tok_whole = key_whole.shape[0]
    cubes_whole = tok_whole // CUBE
    query_cube = cube_means(query_local)
    key_cube, value_cube = cube_means(key_whole), cube_means(value_whole)
    qcube_heads = by_heads(query_cube)
    kcube_heads = by_heads(key_cube)
    vcube_heads = by_heads(value_cube)
    coarse_scores = (
        jnp.einsum("ahd,bhd->hab", qcube_heads, kcube_heads, preferred_element_type=jnp.float32)
        * scaling
    )
    coarse_p = softmax_rows(coarse_scores)
    coarse_half = coarse_p.astype(jnp.bfloat16)
    coarse_out = jnp.einsum(
        "hab,bhd->ahd", coarse_half, vcube_heads, preferred_element_type=jnp.float32
    )
    key_cubes = key_whole.reshape(cubes_whole, CUBE, width)
    value_cubes = value_whole.reshape(cubes_whole, CUBE, width)
    key_pick = key_cubes[picked].reshape(cubes_local, picks_each * CUBE, heads_here, HD)
    value_pick = value_cubes[picked].reshape(cubes_local, picks_each * CUBE, heads_here, HD)
    query_blocks = query_local.reshape(cubes_local, CUBE, heads_here, HD)
    fine_scores = (
        jnp.einsum("cthd,ckhd->chtk", query_blocks, key_pick, preferred_element_type=jnp.float32)
        * scaling
    )
    fine_p = softmax_rows(fine_scores)
    fine_half = fine_p.astype(jnp.bfloat16)
    fine_out = jnp.einsum(
        "chtk,ckhd->cthd", fine_half, value_pick, preferred_element_type=jnp.float32
    )
    attention = (
        (fine_out + coarse_out[:, None, :, :]).astype(jnp.bfloat16).reshape(tok_local, width)
    )
    attention_whole = lax.all_gather(attention, ("ctx", "clip"), axis=0, tiled=True)
    grad_cube = jnp.sum(
        attn_grad.astype(jnp.float32).reshape(cubes_local, CUBE, width), axis=1
    ).astype(jnp.bfloat16)
    gcube_heads = by_heads(grad_cube)
    coarse_dp = jnp.einsum(
        "ahd,bhd->hab", gcube_heads, vcube_heads, preferred_element_type=jnp.float32
    )
    coarse_delta = jnp.sum(coarse_p * coarse_dp, axis=-1, keepdims=True)
    coarse_ds = (scaling * coarse_p * (coarse_dp - coarse_delta)).astype(jnp.bfloat16)
    coarse_dq = jnp.einsum(
        "hab,bhd->ahd", coarse_ds, kcube_heads, preferred_element_type=jnp.float32
    )
    coarse_dk = jnp.einsum(
        "hab,ahd->bhd", coarse_ds, qcube_heads, preferred_element_type=jnp.float32
    )
    coarse_dv = jnp.einsum(
        "hab,ahd->bhd", coarse_half, gcube_heads, preferred_element_type=jnp.float32
    )
    cube_terms = (
        jnp.concatenate(
            [coarse_dk.reshape(cubes_whole, width), coarse_dv.reshape(cubes_whole, width)], axis=1
        )
        / CUBE
    )
    grad_blocks = attn_grad.reshape(cubes_local, CUBE, heads_here, HD)
    fine_dp = jnp.einsum(
        "cthd,ckhd->chtk", grad_blocks, value_pick, preferred_element_type=jnp.float32
    )
    fine_delta = jnp.sum(fine_p * fine_dp, axis=-1, keepdims=True)
    fine_ds = (scaling * fine_p * (fine_dp - fine_delta)).astype(jnp.bfloat16)
    query_grad = jnp.einsum(
        "chtk,ckhd->cthd", fine_ds, key_pick, preferred_element_type=jnp.float32
    )
    query_grad = (query_grad + coarse_dq[:, None, :, :] / CUBE).astype(jnp.bfloat16)
    query_grad = query_grad.reshape(tok_local, width)
    key_picked = jnp.einsum(
        "chtk,cthd->ckhd", fine_ds, query_blocks, preferred_element_type=jnp.float32
    )
    value_picked = jnp.einsum(
        "chtk,cthd->ckhd", fine_half, grad_blocks, preferred_element_type=jnp.float32
    )
    flat_terms = jnp.concatenate(
        [
            key_picked.reshape(cubes_local, picks_each, CUBE, width),
            value_picked.reshape(cubes_local, picks_each, CUBE, width),
        ],
        axis=3,
    )
    flat_terms = flat_terms.reshape(cubes_local * picks_each, CUBE, 2 * width)
    picked_flat = picked.reshape(-1)
    running = jnp.broadcast_to(cube_terms[:, None, :], (cubes_whole, CUBE, 2 * width))
    running = running.at[picked_flat].add(flat_terms)
    summed = lax.psum_scatter(
        running.reshape(tok_whole, 2 * width).astype(jnp.bfloat16),
        "ctx",
        scatter_dimension=0,
        tiled=True,
    ).astype(jnp.float32)
    key_grad = summed[:, :width].astype(jnp.bfloat16)
    value_grad = summed[:, width:].astype(jnp.bfloat16)
    weight_grad = lax.dot_general(
        attention_whole, columns_whole, (((0,), (0,)), ((), ())), preferred_element_type=jnp.float32
    ).astype(jnp.bfloat16)
    return (attention[None], query_grad[None], key_grad[None], value_grad[None], weight_grad)

ROWS = 16
LOW = -1e30


def dot_nt(a, b):
    return lax.dot_general(a, b, (((1,), (1,)), ((), ())), preferred_element_type=jnp.float32)


def dot_nn(a, b):
    return lax.dot_general(a, b, (((1,), (0,)), ((), ())), preferred_element_type=jnp.float32)


def dot_tn(a, b):
    return lax.dot_general(a, b, (((0,), (0,)), ((), ())), preferred_element_type=jnp.float32)


def cube_rows(blocks, factor):
    at_row = lax.broadcasted_iota(jnp.int32, (ROWS, blocks.shape[1]), 0)
    rows = jnp.zeros((ROWS, blocks.shape[1]), jnp.float32)
    for cube in range(blocks.shape[0] // CUBE):
        part = blocks[cube * CUBE : (cube + 1) * CUBE].astype(jnp.float32)
        total = jnp.sum(part, axis=0, keepdims=True) * factor
        rows = jnp.where(at_row == cube, total, rows)
    return rows.astype(jnp.bfloat16)


def over_tokens(rows, cubes):
    return jnp.concatenate(
        [jnp.broadcast_to(rows[cube : cube + 1], (CUBE, rows.shape[1])) for cube in range(cubes)],
        axis=0,
    )


def pair_kernel(
    n_clip, n_head, chosen_in, query_in, key, value, layer, weight,
    attention_out, query_grad_out, key_grad_out, value_grad_out, weight_grad_out,
    attention, query_grad, key_grad, value_grad, weight_grad, chosen, query, keys, values, columns, held_weight, weight_t, fine, coarse, turned,
    partial, partial_in, grad, terms, terms_in,
    kv_sem, deal_sem, share_sem, across_sem, share_far_sem, part_sem, turn_sem, turn_far_sem,
    term_sem, local_sem, out_sem,
):
    scaling = HD ** (-0.5)
    tokens, width = query_in.shape
    cols = weight.shape[1]
    heads = width // HD
    cubes = tokens // CUBE
    cubes_whole = 2 * cubes
    quarter = tokens // n_head
    x, h, z = lax.axis_index("ctx"), lax.axis_index("head"), lax.axis_index("clip")
    other = 1 - x
    near, over = h + 1 - 2 * lax.rem(h, 2), lax.rem(h + 2, n_head)

    def rows_of(head):
        return pl.ds(pl.multiple_of(head * quarter, quarter), quarter)

    my_rows, over_rows = rows_of(h), rows_of(over)

    def to_clip(step):
        return {"clip": lax.rem(z + step, n_clip)}

    def from_clip(step):
        return lax.rem(z + n_clip - step, n_clip)

    def column_block(clip):
        return pl.ds(pl.multiple_of(clip * cols, cols), cols)

    def slot(ctx, clip):
        return pl.ds(pl.multiple_of((ctx * n_clip + clip) * tokens, tokens), tokens)

    sent, written = [], []

    def write(src, dst):
        copy = pltpu.make_async_copy(src, dst, out_sem.at[len(written)])
        copy.start()
        written.append(copy)

    def send(src, dst, sems, index, device):
        copy = pltpu.make_async_remote_copy(
            src_ref=src, dst_ref=dst,
            send_sem=sems.at[(0,) + index], recv_sem=sems.at[(1,) + index],
            device_id=device, device_id_type=pl.DeviceIdType.MESH,
        )
        copy.start()
        sent.append(copy)
        return copy

    mine = pl.ds(pl.multiple_of(x * tokens, tokens), tokens)
    locals_in = [
        pltpu.make_async_copy(src, dst, local_sem.at[index])
        for index, (src, dst) in enumerate(
            [
                (query_in, query),
                (key, keys.at[mine]),
                (value, values.at[mine]),
                (weight, held_weight),
                (layer.at[:, column_block(z)], columns.at[x, z]),
                (chosen_in, chosen),
            ]
        )
    ]
    for copy in locals_in:
        copy.start()

    barrier = pltpu.get_barrier_semaphore()
    partners = [{"ctx": other}]
    partners += [to_clip(step) for step in range(1, n_clip)]
    partners += [{"head": near}, {"head": over}]
    for partner in partners:
        pl.semaphore_signal(barrier, inc=1, device_id=partner, device_id_type=pl.DeviceIdType.MESH)
    pl.semaphore_wait(barrier, len(partners))

    key_copy = send(key, keys.at[mine], kv_sem, (0,), {"ctx": other})
    value_copy = send(value, values.at[mine], kv_sem, (1,), {"ctx": other})
    deals = [None]
    for step in range(1, n_clip):
        deals.append(
            send(
                layer.at[my_rows, column_block(lax.rem(z + step, n_clip))],
                columns.at[x, z, my_rows], deal_sem, (step,), to_clip(step),
            )
        )
    across = [
        send(
            layer.at[my_rows, column_block(z)], columns.at[x, z, my_rows],
            across_sem, (0,), {"ctx": other},
        )
    ]
    for copy in locals_in:
        copy.wait()
    for head in range(heads):
        at = slice(head * HD, (head + 1) * HD)
        weight_t[:, at] = held_weight[at, :].T
    query_cube = cube_rows(query[...], 1.0 / CUBE)
    column_cube = lax.broadcasted_iota(jnp.int32, (1, cubes_whole * CUBE), 1) // CUBE
    allowed = []
    for cube in range(cubes):
        hit = column_cube == chosen[cube, 0]
        for pick in range(1, chosen.shape[1]):
            hit = hit | (column_cube == chosen[cube, pick])
        allowed.append(jnp.broadcast_to(hit.astype(jnp.float32), (CUBE, cubes_whole * CUBE)))
    allowed = jnp.concatenate(allowed, axis=0) > 0.5
    real = lax.broadcasted_iota(jnp.int32, (ROWS, ROWS), 1) < cubes_whole

    shares = [None]

    def pass_on(step):
        deals[step].wait_recv()
        piece = columns.at[x, from_clip(step), my_rows]
        shares.append(
            [
                send(piece, piece, share_sem, (step, 0), {"head": over}),
                send(piece, piece, share_sem, (step, 1), {"head": near}),
            ]
        )
        across.append(send(piece, piece, across_sem, (step,), {"ctx": other}))

    key_copy.wait_recv()
    value_copy.wait_recv()
    key_cube = cube_rows(keys[...], 1.0 / CUBE)
    value_cube = cube_rows(values[...], 1.0 / CUBE)
    for step in range(1, n_clip):
        pass_on(step)

    early = (heads + 1) // 2
    split = (slice(0, early * HD), slice(early * HD, width))
    turns, turn_far = [], []

    def turn_out(part):
        piece = turned.at[split[part], slot(x, z)]
        turns.append(
            [send(piece, piece, turn_sem, (part, step), to_clip(step)) for step in range(1, n_clip)]
        )

    def turn_across(part, step):
        piece = turned.at[split[part], slot(x, from_clip(step))]
        turn_far.append(send(piece, piece, turn_far_sem, (part, step), {"ctx": other}))

    for head in range(heads):
        at = slice(head * HD, (head + 1) * HD)
        scores = dot_nt(query[:, at], keys[:, at]) * scaling
        scores = jnp.where(allowed, scores, LOW)
        expons = jnp.exp(scores - jnp.max(scores, axis=-1, keepdims=True))
        fine_p = expons / jnp.sum(expons, axis=-1, keepdims=True)
        fine[head] = fine_p
        coarse_scores = dot_nt(query_cube[:, at], key_cube[:, at]) * scaling
        coarse_scores = jnp.where(real, coarse_scores, LOW)
        expons = jnp.exp(coarse_scores - jnp.max(coarse_scores, axis=-1, keepdims=True))
        coarse_p = expons / jnp.sum(expons, axis=-1, keepdims=True)
        coarse[head] = coarse_p
        coarse_out = dot_nn(coarse_p.astype(jnp.bfloat16), value_cube[:, at])
        fine_out = dot_nn(fine_p.astype(jnp.bfloat16), values[:, at])
        result = (fine_out + over_tokens(coarse_out, cubes)).astype(jnp.bfloat16)
        attention[:, at] = result
        turned[at, slot(x, z)] = result.astype(jnp.float32).T.astype(jnp.bfloat16)
        if head == early - 1:
            turn_out(0)
            turn_across(0, 0)
    turn_across(1, 0)
    write(attention, attention_out)

    for step in range(1, n_clip):
        shares[step][0].wait_recv()
        piece = columns.at[x, from_clip(step), over_rows]
        shares[step].append(send(piece, piece, share_sem, (step, 2), {"head": near}))
    parts = [None]
    for step in range(1, n_clip):
        clip = from_clip(step)
        for copy in shares[step][1:]:
            copy.wait_recv()
        partial[step] = dot_nn(columns[x, clip], weight_t[...]).astype(jnp.bfloat16)
        parts.append(
            send(
                partial.at[step], partial_in.at[step], part_sem, (step,),
                {"clip": clip},
            )
        )
    total = dot_nn(columns[x, z], weight_t[...])
    for copy in across:
        copy.wait_recv()
    far = columns.at[other, :, my_rows]
    share_far = [
        send(far, far, share_far_sem, (0,), {"head": over}),
        send(far, far, share_far_sem, (1,), {"head": near}),
    ]
    for step in range(1, n_clip):
        turns[0][step - 1].wait_recv()
        turn_across(0, step)
    share_far[0].wait_recv()
    far = columns.at[other, :, over_rows]
    share_far.append(send(far, far, share_far_sem, (2,), {"head": near}))
    for copy in share_far[1:] + turn_far[:1] + turn_far[2:]:
        copy.wait_recv()

    def weight_rows(part):
        for begin in range(0, cols, tile):
            at = slice(begin, begin + tile)
            block = columns[:, :, :, at].reshape(2 * n_clip * tokens, tile)
            weight_grad[split[part], at] = dot_nn(turned[split[part], :], block).astype(jnp.bfloat16)
        write(weight_grad.at[split[part]], weight_grad_out.at[split[part]])

    tile = 256
    weight_rows(0)
    for step in range(1, n_clip):
        parts[step].wait_recv()
        total = total + partial_in[step].astype(jnp.float32)
    turn_out(1)
    grad[...] = total.astype(jnp.bfloat16)
    grad_cube = cube_rows(grad[...], 1.0)

    term_copies = []
    for head in range(heads):
        at = slice(head * HD, (head + 1) * HD)
        fine_p = fine[head]
        fine_half = fine_p.astype(jnp.bfloat16)
        fine_dp = dot_nt(grad[:, at], values[:, at])
        delta = jnp.sum(fine_p * fine_dp, axis=-1, keepdims=True)
        fine_ds = (scaling * fine_p * (fine_dp - delta)).astype(jnp.bfloat16)
        coarse_p = coarse[head]
        coarse_half = coarse_p.astype(jnp.bfloat16)
        coarse_dp = dot_nt(grad_cube[:, at], value_cube[:, at])
        delta = jnp.sum(coarse_p * coarse_dp, axis=-1, keepdims=True)
        coarse_ds = (scaling * coarse_p * (coarse_dp - delta)).astype(jnp.bfloat16)
        coarse_dq = dot_nn(coarse_ds, key_cube[:, at]) * (1.0 / CUBE)
        coarse_dk = dot_tn(coarse_ds, query_cube[:, at]) * (1.0 / CUBE)
        coarse_dv = dot_tn(coarse_half, grad_cube[:, at]) * (1.0 / CUBE)
        dq = dot_nn(fine_ds, keys[:, at]) + over_tokens(coarse_dq, cubes)
        query_grad[:, at] = dq.astype(jnp.bfloat16)
        dk = dot_tn(fine_ds, query[:, at]) + over_tokens(coarse_dk, cubes_whole)
        dv = dot_tn(fine_half, grad[:, at]) + over_tokens(coarse_dv, cubes_whole)
        dk, dv = dk.astype(jnp.bfloat16), dv.astype(jnp.bfloat16)
        for ctx in range(2):
            terms[ctx, head, 0] = dk[ctx * tokens : (ctx + 1) * tokens]
            terms[ctx, head, 1] = dv[ctx * tokens : (ctx + 1) * tokens]
        term_copies.append(
            send(terms.at[other, head], terms_in.at[head], term_sem, (head,), {"ctx": other})
        )

    write(query_grad, query_grad_out)

    for step in range(1, n_clip):
        turns[1][step - 1].wait_recv()
        turn_across(1, step)
    for copy in turn_far[1:2] + turn_far[-(n_clip - 1) :]:
        copy.wait_recv()
    weight_rows(1)

    for head in range(heads):
        at = slice(head * HD, (head + 1) * HD)
        term_copies[head].wait_recv()
        summed = terms[x, head].astype(jnp.float32) + terms_in[head].astype(jnp.float32)
        key_grad[:, at] = summed[0].astype(jnp.bfloat16)
        value_grad[:, at] = summed[1].astype(jnp.bfloat16)
    write(key_grad, key_grad_out)
    write(value_grad, value_grad_out)
    for copy in sent:
        copy.wait_send()
    for copy in written:
        copy.wait()


def copy_out(*refs):
    sem = refs[-1]
    n_out = len(refs) // 3
    loads = [
        pltpu.make_async_copy(refs[index], refs[2 * n_out + index], sem.at[0, index])
        for index in range(n_out)
    ]
    stores = [
        pltpu.make_async_copy(refs[2 * n_out + index], refs[n_out + index], sem.at[1, index])
        for index in range(n_out)
    ]
    for copy in loads:
        copy.start()
    for load, store in zip(loads, stores):
        load.wait()
        store.start()
    for copy in stores:
        copy.wait()


def paired(n_clip, n_head, queries, key_states, value_states, layer_grad, out_weight, chosen):
    tokens, width = queries.shape[1:]
    cols = out_weight.shape[1]
    heads = width // HD
    half = jnp.bfloat16
    whole = 2 * tokens
    far = pl.BlockSpec(memory_space=pltpu.HBM)
    small = jax.ShapeDtypeStruct((tokens, width), half)
    dma = pltpu.SemaphoreType.DMA
    outs = pl.pallas_call(
        functools.partial(pair_kernel, n_clip, n_head),
        out_shape=(small, small, small, small, jax.ShapeDtypeStruct((width, cols), half)),
        in_specs=[far] * 6,
        out_specs=(far,) * 5,
        scratch_shapes=[pltpu.VMEM((tokens, width), half)] * 4
        + [
            pltpu.VMEM((width, cols), half),
            pltpu.SMEM(chosen.shape[1:], jnp.int32),
            pltpu.VMEM((tokens, width), half),
            pltpu.VMEM((whole, width), half),
            pltpu.VMEM((whole, width), half),
            pltpu.VMEM((2, n_clip, tokens, cols), half),
            pltpu.VMEM((width, cols), half),
            pltpu.VMEM((cols, width), half),
            pltpu.VMEM((heads, tokens, whole), jnp.float32),
            pltpu.VMEM((heads, ROWS, ROWS), jnp.float32),
            pltpu.VMEM((width, 2 * n_clip * tokens), half),
            pltpu.VMEM((n_clip, tokens, width), half),
            pltpu.VMEM((n_clip, tokens, width), half),
            pltpu.VMEM((tokens, width), half),
            pltpu.VMEM((2, heads, 2, tokens, HD), half),
            pltpu.VMEM((heads, 2, tokens, HD), half),
            dma((2, 2)),
            dma((2, n_clip)),
            dma((2, n_clip, n_head)),
            dma((2, n_clip)),
            dma((2, n_head)),
            dma((2, n_clip)),
            dma((2, 2, n_clip)),
            dma((2, 2, n_clip)),
            dma((2, heads)),
            dma((6,)),
            dma((6,)),
        ],
        compiler_params=pltpu.CompilerParams(
            collective_id=0, has_side_effects=True, vmem_limit_bytes=60 * 2**20
        ),
    )(chosen[0], queries[0], key_states[0], value_states[0], layer_grad[0], out_weight)
    outs = pl.pallas_call(
        copy_out,
        out_shape=tuple(jax.ShapeDtypeStruct(out.shape, half) for out in outs),
        in_specs=[far] * 5,
        out_specs=(far,) * 5,
        scratch_shapes=[pltpu.VMEM(out.shape, half) for out in outs] + [dma((2, 5))],
        compiler_params=pltpu.CompilerParams(vmem_limit_bytes=60 * 2**20),
    )(*outs)
    return tuple(out[None] for out in outs[:4]) + (outs[4],)


def solution(mesh):
    clips, heads = mesh.shape["clip"], mesh.shape["head"]
    paired_here = mesh.shape["ctx"] == 2 and heads == 4
    body = functools.partial(paired, clips, heads) if paired_here else on_device
    placed = (
        P("clip", "ctx", "head"),
        P("clip", "ctx", "head"),
        P("clip", "ctx", "head"),
        P("clip", "ctx", None),
        P("head", "clip"),
        P("clip", "ctx", None),
    )
    return jax.shard_map(
        body,
        mesh=mesh,
        in_specs=placed,
        out_specs=(
            P("clip", "ctx", "head"),
            P("clip", "ctx", "head"),
            P("clip", "ctx", "head"),
            P("clip", "ctx", "head"),
            P("head", "clip"),
        ),
        check_vma=False,
    )
```

```python
import functools

import jax
import jax.numpy as jnp
from jax import lax
from jax.experimental import pallas as pl
from jax.experimental.pallas import tpu as pltpu
from jax.sharding import PartitionSpec as P

HD = 128
CUBE = 64


def cube_means(blocks):
    grouped = blocks.astype(jnp.float32).reshape(-1, CUBE, blocks.shape[-1])
    return jnp.mean(grouped, axis=1).astype(jnp.bfloat16)


def by_heads(blocks):
    return blocks.reshape(blocks.shape[0], -1, HD)


def softmax_rows(scores):
    largest = jnp.max(scores, axis=-1, keepdims=True)
    expons = jnp.exp(scores - largest)
    return expons / jnp.sum(expons, axis=-1, keepdims=True)


def on_device(queries, key_states, value_states, layer_grad, out_weight, chosen):
    scaling = HD ** (-0.5)
    query_local = queries[0]
    key_local = key_states[0]
    value_local = value_states[0]
    layer_local = layer_grad[0]
    picked = chosen[0]
    tok_local, width = query_local.shape
    heads_here = width // HD
    cubes_local = tok_local // CUBE
    picks_each = picked.shape[1]
    kv_whole = lax.all_gather(
        jnp.concatenate([key_local, value_local], axis=1), "ctx", axis=0, tiled=True
    )
    key_whole, value_whole = kv_whole[:, :width], kv_whole[:, width:]
    columns = lax.all_to_all(layer_local, "clip", split_axis=1, concat_axis=0, tiled=True)
    grad_parts = lax.dot_general(
        columns, out_weight, (((1,), (1,)), ((), ())), preferred_element_type=jnp.float32
    ).astype(jnp.bfloat16)
    grad_parts = lax.all_to_all(
        grad_parts.reshape(-1, tok_local, width), "clip", split_axis=0, concat_axis=0, tiled=True
    )
    attn_grad = jnp.sum(grad_parts.astype(jnp.float32), axis=0).astype(jnp.bfloat16)
    columns_whole = lax.all_gather(columns, "ctx", axis=0, tiled=True)
    tok_whole = key_whole.shape[0]
    cubes_whole = tok_whole // CUBE
    query_cube = cube_means(query_local)
    key_cube, value_cube = cube_means(key_whole), cube_means(value_whole)
    qcube_heads = by_heads(query_cube)
    kcube_heads = by_heads(key_cube)
    vcube_heads = by_heads(value_cube)
    coarse_scores = (
        jnp.einsum("ahd,bhd->hab", qcube_heads, kcube_heads, preferred_element_type=jnp.float32)
        * scaling
    )
    coarse_p = softmax_rows(coarse_scores)
    coarse_half = coarse_p.astype(jnp.bfloat16)
    coarse_out = jnp.einsum(
        "hab,bhd->ahd", coarse_half, vcube_heads, preferred_element_type=jnp.float32
    )
    key_cubes = key_whole.reshape(cubes_whole, CUBE, width)
    value_cubes = value_whole.reshape(cubes_whole, CUBE, width)
    key_pick = key_cubes[picked].reshape(cubes_local, picks_each * CUBE, heads_here, HD)
    value_pick = value_cubes[picked].reshape(cubes_local, picks_each * CUBE, heads_here, HD)
    query_blocks = query_local.reshape(cubes_local, CUBE, heads_here, HD)
    fine_scores = (
        jnp.einsum("cthd,ckhd->chtk", query_blocks, key_pick, preferred_element_type=jnp.float32)
        * scaling
    )
    fine_p = softmax_rows(fine_scores)
    fine_half = fine_p.astype(jnp.bfloat16)
    fine_out = jnp.einsum(
        "chtk,ckhd->cthd", fine_half, value_pick, preferred_element_type=jnp.float32
    )
    attention = (
        (fine_out + coarse_out[:, None, :, :]).astype(jnp.bfloat16).reshape(tok_local, width)
    )
    attention_whole = lax.all_gather(attention, ("ctx", "clip"), axis=0, tiled=True)
    grad_cube = jnp.sum(
        attn_grad.astype(jnp.float32).reshape(cubes_local, CUBE, width), axis=1
    ).astype(jnp.bfloat16)
    gcube_heads = by_heads(grad_cube)
    coarse_dp = jnp.einsum(
        "ahd,bhd->hab", gcube_heads, vcube_heads, preferred_element_type=jnp.float32
    )
    coarse_delta = jnp.sum(coarse_p * coarse_dp, axis=-1, keepdims=True)
    coarse_ds = (scaling * coarse_p * (coarse_dp - coarse_delta)).astype(jnp.bfloat16)
    coarse_dq = jnp.einsum(
        "hab,bhd->ahd", coarse_ds, kcube_heads, preferred_element_type=jnp.float32
    )
    coarse_dk = jnp.einsum(
        "hab,ahd->bhd", coarse_ds, qcube_heads, preferred_element_type=jnp.float32
    )
    coarse_dv = jnp.einsum(
        "hab,ahd->bhd", coarse_half, gcube_heads, preferred_element_type=jnp.float32
    )
    cube_terms = (
        jnp.concatenate(
            [coarse_dk.reshape(cubes_whole, width), coarse_dv.reshape(cubes_whole, width)], axis=1
        )
        / CUBE
    )
    grad_blocks = attn_grad.reshape(cubes_local, CUBE, heads_here, HD)
    fine_dp = jnp.einsum(
        "cthd,ckhd->chtk", grad_blocks, value_pick, preferred_element_type=jnp.float32
    )
    fine_delta = jnp.sum(fine_p * fine_dp, axis=-1, keepdims=True)
    fine_ds = (scaling * fine_p * (fine_dp - fine_delta)).astype(jnp.bfloat16)
    query_grad = jnp.einsum(
        "chtk,ckhd->cthd", fine_ds, key_pick, preferred_element_type=jnp.float32
    )
    query_grad = (query_grad + coarse_dq[:, None, :, :] / CUBE).astype(jnp.bfloat16)
    query_grad = query_grad.reshape(tok_local, width)
    key_picked = jnp.einsum(
        "chtk,cthd->ckhd", fine_ds, query_blocks, preferred_element_type=jnp.float32
    )
    value_picked = jnp.einsum(
        "chtk,cthd->ckhd", fine_half, grad_blocks, preferred_element_type=jnp.float32
    )
    flat_terms = jnp.concatenate(
        [
            key_picked.reshape(cubes_local, picks_each, CUBE, width),
            value_picked.reshape(cubes_local, picks_each, CUBE, width),
        ],
        axis=3,
    )
    flat_terms = flat_terms.reshape(cubes_local * picks_each, CUBE, 2 * width)
    picked_flat = picked.reshape(-1)
    running = jnp.broadcast_to(cube_terms[:, None, :], (cubes_whole, CUBE, 2 * width))
    running = running.at[picked_flat].add(flat_terms)
    summed = lax.psum_scatter(
        running.reshape(tok_whole, 2 * width).astype(jnp.bfloat16),
        "ctx",
        scatter_dimension=0,
        tiled=True,
    ).astype(jnp.float32)
    key_grad = summed[:, :width].astype(jnp.bfloat16)
    value_grad = summed[:, width:].astype(jnp.bfloat16)
    weight_grad = lax.dot_general(
        attention_whole, columns_whole, (((0,), (0,)), ((), ())), preferred_element_type=jnp.float32
    ).astype(jnp.bfloat16)
    return (attention[None], query_grad[None], key_grad[None], value_grad[None], weight_grad)

ROWS = 16
LOW = -1e30


def dot_nt(a, b):
    return lax.dot_general(a, b, (((1,), (1,)), ((), ())), preferred_element_type=jnp.float32)


def dot_nn(a, b):
    return lax.dot_general(a, b, (((1,), (0,)), ((), ())), preferred_element_type=jnp.float32)


def dot_tn(a, b):
    return lax.dot_general(a, b, (((0,), (0,)), ((), ())), preferred_element_type=jnp.float32)


def cube_rows(blocks, factor):
    at_row = lax.broadcasted_iota(jnp.int32, (ROWS, blocks.shape[1]), 0)
    rows = jnp.zeros((ROWS, blocks.shape[1]), jnp.float32)
    for cube in range(blocks.shape[0] // CUBE):
        part = blocks[cube * CUBE : (cube + 1) * CUBE].astype(jnp.float32)
        total = jnp.sum(part, axis=0, keepdims=True) * factor
        rows = jnp.where(at_row == cube, total, rows)
    return rows.astype(jnp.bfloat16)


def over_tokens(rows, cubes):
    return jnp.concatenate(
        [jnp.broadcast_to(rows[cube : cube + 1], (CUBE, rows.shape[1])) for cube in range(cubes)],
        axis=0,
    )


def pair_kernel(
    n_clip, n_head, chosen_in, query_in, key, value, layer, weight,
    attention_out, query_grad_out, key_grad_out, value_grad_out, weight_grad_out,
    attention, query_grad, key_grad, value_grad, weight_grad, chosen, query, keys, values, columns, held_weight, weight_t, fine, coarse, turned,
    partial, partial_in, grad, terms, terms_in,
    kv_sem, deal_sem, share_sem, across_sem, share_far_sem, part_sem, turn_sem, turn_far_sem,
    term_sem, local_sem, out_sem,
):
    scaling = HD ** (-0.5)
    tokens, width = query_in.shape
    cols = weight.shape[1]
    heads = width // HD
    cubes = tokens // CUBE
    cubes_whole = 2 * cubes
    quarter = tokens // n_head
    x, h, z = lax.axis_index("ctx"), lax.axis_index("head"), lax.axis_index("clip")
    other = 1 - x
    near, over = h + 1 - 2 * lax.rem(h, 2), lax.rem(h + 2, n_head)

    def rows_of(head):
        return pl.ds(pl.multiple_of(head * quarter, quarter), quarter)

    my_rows, over_rows = rows_of(h), rows_of(over)

    def to_clip(step):
        return {"clip": lax.rem(z + step, n_clip)}

    def from_clip(step):
        return lax.rem(z + n_clip - step, n_clip)

    def column_block(clip):
        return pl.ds(pl.multiple_of(clip * cols, cols), cols)

    def slot(ctx, clip):
        return pl.ds(pl.multiple_of((ctx * n_clip + clip) * tokens, tokens), tokens)

    sent, written = [], []

    def write(src, dst):
        copy = pltpu.make_async_copy(src, dst, out_sem.at[len(written)])
        copy.start()
        written.append(copy)

    def send(src, dst, sems, index, device):
        copy = pltpu.make_async_remote_copy(
            src_ref=src, dst_ref=dst,
            send_sem=sems.at[(0,) + index], recv_sem=sems.at[(1,) + index],
            device_id=device, device_id_type=pl.DeviceIdType.MESH,
        )
        copy.start()
        sent.append(copy)
        return copy

    mine = pl.ds(pl.multiple_of(x * tokens, tokens), tokens)
    locals_in = [
        pltpu.make_async_copy(src, dst, local_sem.at[index])
        for index, (src, dst) in enumerate(
            [
                (query_in, query),
                (key, keys.at[mine]),
                (value, values.at[mine]),
                (weight, held_weight),
                (layer.at[:, column_block(z)], columns.at[x, z]),
                (chosen_in, chosen),
            ]
        )
    ]
    for copy in locals_in:
        copy.start()

    barrier = pltpu.get_barrier_semaphore()
    partners = [{"ctx": other}]
    partners += [to_clip(step) for step in range(1, n_clip)]
    partners += [{"head": near}, {"head": over}]
    for partner in partners:
        pl.semaphore_signal(barrier, inc=1, device_id=partner, device_id_type=pl.DeviceIdType.MESH)
    pl.semaphore_wait(barrier, len(partners))

    key_copy = send(key, keys.at[mine], kv_sem, (0,), {"ctx": other})
    value_copy = send(value, values.at[mine], kv_sem, (1,), {"ctx": other})
    deals = [None]
    for step in range(1, n_clip):
        deals.append(
            send(
                layer.at[my_rows, column_block(lax.rem(z + step, n_clip))],
                columns.at[x, z, my_rows], deal_sem, (step,), to_clip(step),
            )
        )
    across = [
        send(
            layer.at[my_rows, column_block(z)], columns.at[x, z, my_rows],
            across_sem, (0,), {"ctx": other},
        )
    ]
    for copy in locals_in:
        copy.wait()
    for head in range(heads):
        at = slice(head * HD, (head + 1) * HD)
        weight_t[:, at] = held_weight[at, :].T
    query_cube = cube_rows(query[...], 1.0 / CUBE)
    column_cube = lax.broadcasted_iota(jnp.int32, (1, cubes_whole * CUBE), 1) // CUBE
    allowed = []
    for cube in range(cubes):
        hit = column_cube == chosen[cube, 0]
        for pick in range(1, chosen.shape[1]):
            hit = hit | (column_cube == chosen[cube, pick])
        allowed.append(jnp.broadcast_to(hit.astype(jnp.float32), (CUBE, cubes_whole * CUBE)))
    allowed = jnp.concatenate(allowed, axis=0) > 0.5
    real = lax.broadcasted_iota(jnp.int32, (ROWS, ROWS), 1) < cubes_whole

    shares = [None]

    def pass_on(step):
        deals[step].wait_recv()
        piece = columns.at[x, from_clip(step), my_rows]
        shares.append(
            [
                send(piece, piece, share_sem, (step, 0), {"head": over}),
                send(piece, piece, share_sem, (step, 1), {"head": near}),
            ]
        )
        across.append(send(piece, piece, across_sem, (step,), {"ctx": other}))

    def hand_on(step):
        shares[step][0].wait_recv()
        piece = columns.at[x, from_clip(step), over_rows]
        shares[step].append(send(piece, piece, share_sem, (step, 2), {"head": near}))

    key_copy.wait_recv()
    key_cube = cube_rows(keys[...], 1.0 / CUBE)
    for head in range(heads):
        at = slice(head * HD, (head + 1) * HD)
        scores = dot_nt(query[:, at], keys[:, at]) * scaling
        scores = jnp.where(allowed, scores, LOW)
        expons = jnp.exp(scores - jnp.max(scores, axis=-1, keepdims=True))
        fine[head] = expons / jnp.sum(expons, axis=-1, keepdims=True)
        coarse_scores = dot_nt(query_cube[:, at], key_cube[:, at]) * scaling
        coarse_scores = jnp.where(real, coarse_scores, LOW)
        expons = jnp.exp(coarse_scores - jnp.max(coarse_scores, axis=-1, keepdims=True))
        coarse[head] = expons / jnp.sum(expons, axis=-1, keepdims=True)

    for step in range(1, n_clip):
        pass_on(step)
    value_copy.wait_recv()
    value_cube = cube_rows(values[...], 1.0 / CUBE)

    early = (heads + 1) // 2
    split = (slice(0, early * HD), slice(early * HD, width))
    turns, turn_far = [], []

    def turn_out(part):
        piece = turned.at[split[part], slot(x, z)]
        turns.append(
            [send(piece, piece, turn_sem, (part, step), to_clip(step)) for step in range(1, n_clip)]
        )

    def turn_across(part, step):
        piece = turned.at[split[part], slot(x, from_clip(step))]
        turn_far.append(send(piece, piece, turn_far_sem, (part, step), {"ctx": other}))

    for head in range(heads):
        at = slice(head * HD, (head + 1) * HD)
        coarse_out = dot_nn(coarse[head].astype(jnp.bfloat16), value_cube[:, at])
        fine_out = dot_nn(fine[head].astype(jnp.bfloat16), values[:, at])
        result = (fine_out + over_tokens(coarse_out, cubes)).astype(jnp.bfloat16)
        attention[:, at] = result
        turned[at, slot(x, z)] = result.astype(jnp.float32).T.astype(jnp.bfloat16)
        if head == early - 1:
            turn_out(0)
            turn_across(0, 0)
            for step in range(1, n_clip):
                hand_on(step)
    turn_across(1, 0)
    write(attention, attention_out)

    parts = [None]
    for step in range(1, n_clip):
        clip = from_clip(step)
        for copy in shares[step][1:]:
            copy.wait_recv()
        partial[step] = dot_nn(columns[x, clip], weight_t[...]).astype(jnp.bfloat16)
        parts.append(
            send(
                partial.at[step], partial_in.at[step], part_sem, (step,),
                {"clip": clip},
            )
        )
    total = dot_nn(columns[x, z], weight_t[...])
    for copy in across:
        copy.wait_recv()
    far = columns.at[other, :, my_rows]
    share_far = [
        send(far, far, share_far_sem, (0,), {"head": over}),
        send(far, far, share_far_sem, (1,), {"head": near}),
    ]
    for step in range(1, n_clip):
        turns[0][step - 1].wait_recv()
        turn_across(0, step)
    share_far[0].wait_recv()
    far = columns.at[other, :, over_rows]
    share_far.append(send(far, far, share_far_sem, (2,), {"head": near}))
    for copy in share_far[1:] + turn_far[:1] + turn_far[2:]:
        copy.wait_recv()

    def weight_rows(part):
        for begin in range(0, cols, tile):
            at = slice(begin, begin + tile)
            block = columns[:, :, :, at].reshape(2 * n_clip * tokens, tile)
            weight_grad[split[part], at] = dot_nn(turned[split[part], :], block).astype(jnp.bfloat16)
        write(weight_grad.at[split[part]], weight_grad_out.at[split[part]])

    tile = 256
    weight_rows(0)
    for step in range(1, n_clip):
        parts[step].wait_recv()
        total = total + partial_in[step].astype(jnp.float32)
    turn_out(1)
    grad[...] = total.astype(jnp.bfloat16)
    grad_cube = cube_rows(grad[...], 1.0)

    term_copies = []
    for head in range(heads):
        at = slice(head * HD, (head + 1) * HD)
        fine_p = fine[head]
        fine_half = fine_p.astype(jnp.bfloat16)
        fine_dp = dot_nt(grad[:, at], values[:, at])
        delta = jnp.sum(fine_p * fine_dp, axis=-1, keepdims=True)
        fine_ds = (scaling * fine_p * (fine_dp - delta)).astype(jnp.bfloat16)
        coarse_p = coarse[head]
        coarse_half = coarse_p.astype(jnp.bfloat16)
        coarse_dp = dot_nt(grad_cube[:, at], value_cube[:, at])
        delta = jnp.sum(coarse_p * coarse_dp, axis=-1, keepdims=True)
        coarse_ds = (scaling * coarse_p * (coarse_dp - delta)).astype(jnp.bfloat16)
        coarse_dq = dot_nn(coarse_ds, key_cube[:, at]) * (1.0 / CUBE)
        coarse_dk = dot_tn(coarse_ds, query_cube[:, at]) * (1.0 / CUBE)
        coarse_dv = dot_tn(coarse_half, grad_cube[:, at]) * (1.0 / CUBE)
        dq = dot_nn(fine_ds, keys[:, at]) + over_tokens(coarse_dq, cubes)
        query_grad[:, at] = dq.astype(jnp.bfloat16)
        dk = dot_tn(fine_ds, query[:, at]) + over_tokens(coarse_dk, cubes_whole)
        dv = dot_tn(fine_half, grad[:, at]) + over_tokens(coarse_dv, cubes_whole)
        dk, dv = dk.astype(jnp.bfloat16), dv.astype(jnp.bfloat16)
        for ctx in range(2):
            terms[ctx, head, 0] = dk[ctx * tokens : (ctx + 1) * tokens]
            terms[ctx, head, 1] = dv[ctx * tokens : (ctx + 1) * tokens]
        term_copies.append(
            send(terms.at[other, head], terms_in.at[head], term_sem, (head,), {"ctx": other})
        )

    write(query_grad, query_grad_out)

    for step in range(1, n_clip):
        turns[1][step - 1].wait_recv()
        turn_across(1, step)
    for head in range(heads):
        at = slice(head * HD, (head + 1) * HD)
        term_copies[head].wait_recv()
        summed = terms[x, head].astype(jnp.float32) + terms_in[head].astype(jnp.float32)
        key_grad[:, at] = summed[0].astype(jnp.bfloat16)
        value_grad[:, at] = summed[1].astype(jnp.bfloat16)
    write(key_grad, key_grad_out)
    write(value_grad, value_grad_out)
    for copy in turn_far[1:2] + turn_far[-(n_clip - 1) :]:
        copy.wait_recv()
    weight_rows(1)
    for copy in sent:
        copy.wait_send()
    for copy in written:
        copy.wait()


def copy_out(*refs):
    sem = refs[-1]
    n_out = len(refs) // 3
    loads = [
        pltpu.make_async_copy(refs[index], refs[2 * n_out + index], sem.at[0, index])
        for index in range(n_out)
    ]
    stores = [
        pltpu.make_async_copy(refs[2 * n_out + index], refs[n_out + index], sem.at[1, index])
        for index in range(n_out)
    ]
    for copy in loads:
        copy.start()
    for load, store in zip(loads, stores):
        load.wait()
        store.start()
    for copy in stores:
        copy.wait()


def paired(n_clip, n_head, queries, key_states, value_states, layer_grad, out_weight, chosen):
    tokens, width = queries.shape[1:]
    cols = out_weight.shape[1]
    heads = width // HD
    half = jnp.bfloat16
    whole = 2 * tokens
    far = pl.BlockSpec(memory_space=pltpu.HBM)
    small = jax.ShapeDtypeStruct((tokens, width), half)
    dma = pltpu.SemaphoreType.DMA
    outs = pl.pallas_call(
        functools.partial(pair_kernel, n_clip, n_head),
        out_shape=(small, small, small, small, jax.ShapeDtypeStruct((width, cols), half)),
        in_specs=[far] * 6,
        out_specs=(far,) * 5,
        scratch_shapes=[pltpu.VMEM((tokens, width), half)] * 4
        + [
            pltpu.VMEM((width, cols), half),
            pltpu.SMEM(chosen.shape[1:], jnp.int32),
            pltpu.VMEM((tokens, width), half),
            pltpu.VMEM((whole, width), half),
            pltpu.VMEM((whole, width), half),
            pltpu.VMEM((2, n_clip, tokens, cols), half),
            pltpu.VMEM((width, cols), half),
            pltpu.VMEM((cols, width), half),
            pltpu.VMEM((heads, tokens, whole), jnp.float32),
            pltpu.VMEM((heads, ROWS, ROWS), jnp.float32),
            pltpu.VMEM((width, 2 * n_clip * tokens), half),
            pltpu.VMEM((n_clip, tokens, width), half),
            pltpu.VMEM((n_clip, tokens, width), half),
            pltpu.VMEM((tokens, width), half),
            pltpu.VMEM((2, heads, 2, tokens, HD), half),
            pltpu.VMEM((heads, 2, tokens, HD), half),
            dma((2, 2)),
            dma((2, n_clip)),
            dma((2, n_clip, n_head)),
            dma((2, n_clip)),
            dma((2, n_head)),
            dma((2, n_clip)),
            dma((2, 2, n_clip)),
            dma((2, 2, n_clip)),
            dma((2, heads)),
            dma((6,)),
            dma((6,)),
        ],
        compiler_params=pltpu.CompilerParams(
            collective_id=0, has_side_effects=True, vmem_limit_bytes=60 * 2**20
        ),
    )(chosen[0], queries[0], key_states[0], value_states[0], layer_grad[0], out_weight)
    outs = pl.pallas_call(
        copy_out,
        out_shape=tuple(jax.ShapeDtypeStruct(out.shape, half) for out in outs),
        in_specs=[far] * 5,
        out_specs=(far,) * 5,
        scratch_shapes=[pltpu.VMEM(out.shape, half) for out in outs] + [dma((2, 5))],
        compiler_params=pltpu.CompilerParams(vmem_limit_bytes=60 * 2**20),
    )(*outs)
    return tuple(out[None] for out in outs[:4]) + (outs[4],)


def solution(mesh):
    clips, heads = mesh.shape["clip"], mesh.shape["head"]
    paired_here = mesh.shape["ctx"] == 2 and heads == 4
    body = functools.partial(paired, clips, heads) if paired_here else on_device
    placed = (
        P("clip", "ctx", "head"),
        P("clip", "ctx", "head"),
        P("clip", "ctx", "head"),
        P("clip", "ctx", None),
        P("head", "clip"),
        P("clip", "ctx", None),
    )
    return jax.shard_map(
        body,
        mesh=mesh,
        in_specs=placed,
        out_specs=(
            P("clip", "ctx", "head"),
            P("clip", "ctx", "head"),
            P("clip", "ctx", "head"),
            P("clip", "ctx", "head"),
            P("head", "clip"),
        ),
        check_vma=False,
    )
```

```python
import functools

import jax
import jax.numpy as jnp
from jax import lax
from jax.experimental import pallas as pl
from jax.experimental.pallas import tpu as pltpu
from jax.sharding import PartitionSpec as P

HD = 128
CUBE = 64


def cube_means(blocks):
    grouped = blocks.astype(jnp.float32).reshape(-1, CUBE, blocks.shape[-1])
    return jnp.mean(grouped, axis=1).astype(jnp.bfloat16)


def by_heads(blocks):
    return blocks.reshape(blocks.shape[0], -1, HD)


def softmax_rows(scores):
    largest = jnp.max(scores, axis=-1, keepdims=True)
    expons = jnp.exp(scores - largest)
    return expons / jnp.sum(expons, axis=-1, keepdims=True)


def on_device(queries, key_states, value_states, layer_grad, out_weight, chosen):
    scaling = HD ** (-0.5)
    query_local = queries[0]
    key_local = key_states[0]
    value_local = value_states[0]
    layer_local = layer_grad[0]
    picked = chosen[0]
    tok_local, width = query_local.shape
    heads_here = width // HD
    cubes_local = tok_local // CUBE
    picks_each = picked.shape[1]
    kv_whole = lax.all_gather(
        jnp.concatenate([key_local, value_local], axis=1), "ctx", axis=0, tiled=True
    )
    key_whole, value_whole = kv_whole[:, :width], kv_whole[:, width:]
    columns = lax.all_to_all(layer_local, "clip", split_axis=1, concat_axis=0, tiled=True)
    grad_parts = lax.dot_general(
        columns, out_weight, (((1,), (1,)), ((), ())), preferred_element_type=jnp.float32
    ).astype(jnp.bfloat16)
    grad_parts = lax.all_to_all(
        grad_parts.reshape(-1, tok_local, width), "clip", split_axis=0, concat_axis=0, tiled=True
    )
    attn_grad = jnp.sum(grad_parts.astype(jnp.float32), axis=0).astype(jnp.bfloat16)
    columns_whole = lax.all_gather(columns, "ctx", axis=0, tiled=True)
    tok_whole = key_whole.shape[0]
    cubes_whole = tok_whole // CUBE
    query_cube = cube_means(query_local)
    key_cube, value_cube = cube_means(key_whole), cube_means(value_whole)
    qcube_heads = by_heads(query_cube)
    kcube_heads = by_heads(key_cube)
    vcube_heads = by_heads(value_cube)
    coarse_scores = (
        jnp.einsum("ahd,bhd->hab", qcube_heads, kcube_heads, preferred_element_type=jnp.float32)
        * scaling
    )
    coarse_p = softmax_rows(coarse_scores)
    coarse_half = coarse_p.astype(jnp.bfloat16)
    coarse_out = jnp.einsum(
        "hab,bhd->ahd", coarse_half, vcube_heads, preferred_element_type=jnp.float32
    )
    key_cubes = key_whole.reshape(cubes_whole, CUBE, width)
    value_cubes = value_whole.reshape(cubes_whole, CUBE, width)
    key_pick = key_cubes[picked].reshape(cubes_local, picks_each * CUBE, heads_here, HD)
    value_pick = value_cubes[picked].reshape(cubes_local, picks_each * CUBE, heads_here, HD)
    query_blocks = query_local.reshape(cubes_local, CUBE, heads_here, HD)
    fine_scores = (
        jnp.einsum("cthd,ckhd->chtk", query_blocks, key_pick, preferred_element_type=jnp.float32)
        * scaling
    )
    fine_p = softmax_rows(fine_scores)
    fine_half = fine_p.astype(jnp.bfloat16)
    fine_out = jnp.einsum(
        "chtk,ckhd->cthd", fine_half, value_pick, preferred_element_type=jnp.float32
    )
    attention = (
        (fine_out + coarse_out[:, None, :, :]).astype(jnp.bfloat16).reshape(tok_local, width)
    )
    attention_whole = lax.all_gather(attention, ("ctx", "clip"), axis=0, tiled=True)
    grad_cube = jnp.sum(
        attn_grad.astype(jnp.float32).reshape(cubes_local, CUBE, width), axis=1
    ).astype(jnp.bfloat16)
    gcube_heads = by_heads(grad_cube)
    coarse_dp = jnp.einsum(
        "ahd,bhd->hab", gcube_heads, vcube_heads, preferred_element_type=jnp.float32
    )
    coarse_delta = jnp.sum(coarse_p * coarse_dp, axis=-1, keepdims=True)
    coarse_ds = (scaling * coarse_p * (coarse_dp - coarse_delta)).astype(jnp.bfloat16)
    coarse_dq = jnp.einsum(
        "hab,bhd->ahd", coarse_ds, kcube_heads, preferred_element_type=jnp.float32
    )
    coarse_dk = jnp.einsum(
        "hab,ahd->bhd", coarse_ds, qcube_heads, preferred_element_type=jnp.float32
    )
    coarse_dv = jnp.einsum(
        "hab,ahd->bhd", coarse_half, gcube_heads, preferred_element_type=jnp.float32
    )
    cube_terms = (
        jnp.concatenate(
            [coarse_dk.reshape(cubes_whole, width), coarse_dv.reshape(cubes_whole, width)], axis=1
        )
        / CUBE
    )
    grad_blocks = attn_grad.reshape(cubes_local, CUBE, heads_here, HD)
    fine_dp = jnp.einsum(
        "cthd,ckhd->chtk", grad_blocks, value_pick, preferred_element_type=jnp.float32
    )
    fine_delta = jnp.sum(fine_p * fine_dp, axis=-1, keepdims=True)
    fine_ds = (scaling * fine_p * (fine_dp - fine_delta)).astype(jnp.bfloat16)
    query_grad = jnp.einsum(
        "chtk,ckhd->cthd", fine_ds, key_pick, preferred_element_type=jnp.float32
    )
    query_grad = (query_grad + coarse_dq[:, None, :, :] / CUBE).astype(jnp.bfloat16)
    query_grad = query_grad.reshape(tok_local, width)
    key_picked = jnp.einsum(
        "chtk,cthd->ckhd", fine_ds, query_blocks, preferred_element_type=jnp.float32
    )
    value_picked = jnp.einsum(
        "chtk,cthd->ckhd", fine_half, grad_blocks, preferred_element_type=jnp.float32
    )
    flat_terms = jnp.concatenate(
        [
            key_picked.reshape(cubes_local, picks_each, CUBE, width),
            value_picked.reshape(cubes_local, picks_each, CUBE, width),
        ],
        axis=3,
    )
    flat_terms = flat_terms.reshape(cubes_local * picks_each, CUBE, 2 * width)
    picked_flat = picked.reshape(-1)
    running = jnp.broadcast_to(cube_terms[:, None, :], (cubes_whole, CUBE, 2 * width))
    running = running.at[picked_flat].add(flat_terms)
    summed = lax.psum_scatter(
        running.reshape(tok_whole, 2 * width).astype(jnp.bfloat16),
        "ctx",
        scatter_dimension=0,
        tiled=True,
    ).astype(jnp.float32)
    key_grad = summed[:, :width].astype(jnp.bfloat16)
    value_grad = summed[:, width:].astype(jnp.bfloat16)
    weight_grad = lax.dot_general(
        attention_whole, columns_whole, (((0,), (0,)), ((), ())), preferred_element_type=jnp.float32
    ).astype(jnp.bfloat16)
    return (attention[None], query_grad[None], key_grad[None], value_grad[None], weight_grad)

ROWS = 16
LOW = -1e30


def dot_nt(a, b):
    return lax.dot_general(a, b, (((1,), (1,)), ((), ())), preferred_element_type=jnp.float32)


def dot_nn(a, b):
    return lax.dot_general(a, b, (((1,), (0,)), ((), ())), preferred_element_type=jnp.float32)


def dot_tn(a, b):
    return lax.dot_general(a, b, (((0,), (0,)), ((), ())), preferred_element_type=jnp.float32)


def cube_rows(blocks, factor):
    at_row = lax.broadcasted_iota(jnp.int32, (ROWS, blocks.shape[1]), 0)
    rows = jnp.zeros((ROWS, blocks.shape[1]), jnp.float32)
    for cube in range(blocks.shape[0] // CUBE):
        part = blocks[cube * CUBE : (cube + 1) * CUBE].astype(jnp.float32)
        total = jnp.sum(part, axis=0, keepdims=True) * factor
        rows = jnp.where(at_row == cube, total, rows)
    return rows.astype(jnp.bfloat16)


def over_tokens(rows, cubes):
    return jnp.concatenate(
        [jnp.broadcast_to(rows[cube : cube + 1], (CUBE, rows.shape[1])) for cube in range(cubes)],
        axis=0,
    )


def pair_kernel(
    n_clip, n_head, chosen_in, query_in, key, value, layer, weight,
    attention_out, query_grad_out, key_grad_out, value_grad_out, weight_grad_out,
    attention, query_grad, key_grad, value_grad, weight_grad, chosen, query, keys, values, columns, held_weight, weight_t, fine, coarse, turned,
    partial, partial_in, grad, terms, terms_in,
    kv_sem, deal_sem, share_sem, across_sem, share_far_sem, part_sem, turn_sem, turn_far_sem,
    term_sem, local_sem, out_sem,
):
    scaling = HD ** (-0.5)
    tokens, width = query_in.shape
    cols = weight.shape[1]
    heads = width // HD
    cubes = tokens // CUBE
    cubes_whole = 2 * cubes
    quarter = tokens // n_head
    x, h, z = lax.axis_index("ctx"), lax.axis_index("head"), lax.axis_index("clip")
    other = 1 - x
    near, over = h + 1 - 2 * lax.rem(h, 2), lax.rem(h + 2, n_head)

    def rows_of(head):
        return pl.ds(pl.multiple_of(head * quarter, quarter), quarter)

    my_rows, over_rows = rows_of(h), rows_of(over)

    def to_clip(step):
        return {"clip": lax.rem(z + step, n_clip)}

    def from_clip(step):
        return lax.rem(z + n_clip - step, n_clip)

    def column_block(clip):
        return pl.ds(pl.multiple_of(clip * cols, cols), cols)

    def slot(ctx, clip):
        return pl.ds(pl.multiple_of((ctx * n_clip + clip) * tokens, tokens), tokens)

    sent, written = [], []

    def write(src, dst):
        copy = pltpu.make_async_copy(src, dst, out_sem.at[len(written)])
        copy.start()
        written.append(copy)

    def send(src, dst, sems, index, device):
        copy = pltpu.make_async_remote_copy(
            src_ref=src, dst_ref=dst,
            send_sem=sems.at[(0,) + index], recv_sem=sems.at[(1,) + index],
            device_id=device, device_id_type=pl.DeviceIdType.MESH,
        )
        copy.start()
        sent.append(copy)
        return copy

    mine = pl.ds(pl.multiple_of(x * tokens, tokens), tokens)
    locals_in = [
        pltpu.make_async_copy(src, dst, local_sem.at[index])
        for index, (src, dst) in enumerate(
            [
                (query_in, query),
                (key, keys.at[mine]),
                (value, values.at[mine]),
                (weight, held_weight),
                (layer.at[:, column_block(z)], columns.at[x, z]),
                (chosen_in, chosen),
            ]
        )
    ]
    for copy in locals_in:
        copy.start()

    barrier = pltpu.get_barrier_semaphore()
    partners = [{"ctx": other}]
    partners += [to_clip(step) for step in range(1, n_clip)]
    partners += [{"head": near}, {"head": over}]
    for partner in partners:
        pl.semaphore_signal(barrier, inc=1, device_id=partner, device_id_type=pl.DeviceIdType.MESH)
    pl.semaphore_wait(barrier, len(partners))

    key_copy = send(key, keys.at[mine], kv_sem, (0,), {"ctx": other})
    value_copy = send(value, values.at[mine], kv_sem, (1,), {"ctx": other})
    deals = [None]
    for step in range(1, n_clip):
        deals.append(
            send(
                layer.at[my_rows, column_block(lax.rem(z + step, n_clip))],
                columns.at[x, z, my_rows], deal_sem, (step,), to_clip(step),
            )
        )
    across = [
        send(
            layer.at[my_rows, column_block(z)], columns.at[x, z, my_rows],
            across_sem, (0,), {"ctx": other},
        )
    ]
    for copy in locals_in:
        copy.wait()
    for head in range(heads):
        at = slice(head * HD, (head + 1) * HD)
        weight_t[:, at] = held_weight[at, :].T
    query_cube = cube_rows(query[...], 1.0 / CUBE)
    column_cube = lax.broadcasted_iota(jnp.int32, (1, cubes_whole * CUBE), 1) // CUBE
    allowed = []
    for cube in range(cubes):
        hit = column_cube == chosen[cube, 0]
        for pick in range(1, chosen.shape[1]):
            hit = hit | (column_cube == chosen[cube, pick])
        allowed.append(jnp.broadcast_to(hit.astype(jnp.float32), (CUBE, cubes_whole * CUBE)))
    allowed = jnp.concatenate(allowed, axis=0) > 0.5
    real = lax.broadcasted_iota(jnp.int32, (ROWS, ROWS), 1) < cubes_whole

    shares = [None]

    def pass_on(step):
        deals[step].wait_recv()
        piece = columns.at[x, from_clip(step), my_rows]
        shares.append(
            [
                send(piece, piece, share_sem, (step, 0), {"head": over}),
                send(piece, piece, share_sem, (step, 1), {"head": near}),
            ]
        )
        across.append(send(piece, piece, across_sem, (step,), {"ctx": other}))

    def hand_on(step):
        shares[step][0].wait_recv()
        piece = columns.at[x, from_clip(step), over_rows]
        shares[step].append(send(piece, piece, share_sem, (step, 2), {"head": near}))

    key_copy.wait_recv()
    key_cube = cube_rows(keys[...], 1.0 / CUBE)
    for head in range(heads):
        at = slice(head * HD, (head + 1) * HD)
        scores = dot_nt(query[:, at], keys[:, at]) * scaling
        scores = jnp.where(allowed, scores, LOW)
        expons = jnp.exp(scores - jnp.max(scores, axis=-1, keepdims=True))
        fine[head] = expons / jnp.sum(expons, axis=-1, keepdims=True)
        coarse_scores = dot_nt(query_cube[:, at], key_cube[:, at]) * scaling
        coarse_scores = jnp.where(real, coarse_scores, LOW)
        expons = jnp.exp(coarse_scores - jnp.max(coarse_scores, axis=-1, keepdims=True))
        coarse[head] = expons / jnp.sum(expons, axis=-1, keepdims=True)

    for step in range(1, n_clip):
        pass_on(step)
    value_copy.wait_recv()
    value_cube = cube_rows(values[...], 1.0 / CUBE)

    early = (heads + 1) // 2
    split = (slice(0, early * HD), slice(early * HD, width))
    turns, turn_far = [], []

    relayed = n_clip == 4
    ends = (z == 0) | (z == n_clip - 1)
    far_end = n_clip - 1 - lax.rem(z + 2, n_clip)

    def end_to_end(step):
        return ends & (lax.rem(z + step, n_clip) == n_clip - 1 - z)

    def turn_relayed():
        piece = turned.at[split[0], slot(x, z)]
        copies = []
        for step in range(1, n_clip):
            copy = pltpu.make_async_remote_copy(
                src_ref=piece, dst_ref=piece,
                send_sem=turn_sem.at[0, 0, step], recv_sem=turn_sem.at[1, 0, step],
                device_id=to_clip(step), device_id_type=pl.DeviceIdType.MESH,
            )
            pl.when(jnp.logical_not(end_to_end(step)))(copy.start)
            copies.append(copy)
        turns.append(copies)

    def relay():
        source = lax.rem(z + 2, n_clip)
        piece = turned.at[split[0], slot(x, source)]
        step = lax.rem(far_end - source + n_clip, n_clip)
        return pltpu.make_async_remote_copy(
            src_ref=piece, dst_ref=piece,
            send_sem=turn_sem.at[0, 0, 0], recv_sem=turn_sem.at[1, 0, step],
            device_id={"clip": far_end}, device_id_type=pl.DeviceIdType.MESH,
        )

    def turn_out(part):
        if part == 0 and relayed:
            turn_relayed()
            return
        piece = turned.at[split[part], slot(x, z)]
        turns.append(
            [send(piece, piece, turn_sem, (part, step), to_clip(step)) for step in range(1, n_clip)]
        )

    def turn_across(part, step):
        piece = turned.at[split[part], slot(x, from_clip(step))]
        turn_far.append(send(piece, piece, turn_far_sem, (part, step), {"ctx": other}))

    for head in range(heads):
        at = slice(head * HD, (head + 1) * HD)
        coarse_out = dot_nn(coarse[head].astype(jnp.bfloat16), value_cube[:, at])
        fine_out = dot_nn(fine[head].astype(jnp.bfloat16), values[:, at])
        result = (fine_out + over_tokens(coarse_out, cubes)).astype(jnp.bfloat16)
        attention[:, at] = result
        turned[at, slot(x, z)] = result.astype(jnp.float32).T.astype(jnp.bfloat16)
        if head == early - 1:
            turn_out(0)
            turn_across(0, 0)
            for step in range(1, n_clip):
                hand_on(step)
    turn_across(1, 0)
    write(attention, attention_out)

    parts = [None]
    for step in range(1, n_clip):
        clip = from_clip(step)
        for copy in shares[step][1:]:
            copy.wait_recv()
        partial[step] = dot_nn(columns[x, clip], weight_t[...]).astype(jnp.bfloat16)
        parts.append(
            send(
                partial.at[step], partial_in.at[step], part_sem, (step,),
                {"clip": clip},
            )
        )
    total = dot_nn(columns[x, z], weight_t[...])
    for copy in across:
        copy.wait_recv()
    far = columns.at[other, :, my_rows]
    share_far = [
        send(far, far, share_far_sem, (0,), {"head": over}),
        send(far, far, share_far_sem, (1,), {"head": near}),
    ]
    for step in [2, 1, 3] if relayed else range(1, n_clip):
        turns[0][step - 1].wait_recv()
        if relayed and step == 2:
            pl.when(jnp.logical_not(ends))(lambda: relay().start())
        turn_across(0, step)
    share_far[0].wait_recv()
    far = columns.at[other, :, over_rows]
    share_far.append(send(far, far, share_far_sem, (2,), {"head": near}))
    for copy in share_far[1:] + turn_far[:1] + turn_far[2:]:
        copy.wait_recv()

    def weight_rows(part):
        for begin in range(0, cols, tile):
            at = slice(begin, begin + tile)
            block = columns[:, :, :, at].reshape(2 * n_clip * tokens, tile)
            weight_grad[split[part], at] = dot_nn(turned[split[part], :], block).astype(jnp.bfloat16)
        write(weight_grad.at[split[part]], weight_grad_out.at[split[part]])

    tile = 256
    weight_rows(0)
    for step in range(1, n_clip):
        parts[step].wait_recv()
        total = total + partial_in[step].astype(jnp.float32)
    turn_out(1)
    grad[...] = total.astype(jnp.bfloat16)
    grad_cube = cube_rows(grad[...], 1.0)

    term_copies = []
    for head in range(heads):
        at = slice(head * HD, (head + 1) * HD)
        fine_p = fine[head]
        fine_half = fine_p.astype(jnp.bfloat16)
        fine_dp = dot_nt(grad[:, at], values[:, at])
        delta = jnp.sum(fine_p * fine_dp, axis=-1, keepdims=True)
        fine_ds = (scaling * fine_p * (fine_dp - delta)).astype(jnp.bfloat16)
        coarse_p = coarse[head]
        coarse_half = coarse_p.astype(jnp.bfloat16)
        coarse_dp = dot_nt(grad_cube[:, at], value_cube[:, at])
        delta = jnp.sum(coarse_p * coarse_dp, axis=-1, keepdims=True)
        coarse_ds = (scaling * coarse_p * (coarse_dp - delta)).astype(jnp.bfloat16)
        coarse_dq = dot_nn(coarse_ds, key_cube[:, at]) * (1.0 / CUBE)
        coarse_dk = dot_tn(coarse_ds, query_cube[:, at]) * (1.0 / CUBE)
        coarse_dv = dot_tn(coarse_half, grad_cube[:, at]) * (1.0 / CUBE)
        dq = dot_nn(fine_ds, keys[:, at]) + over_tokens(coarse_dq, cubes)
        query_grad[:, at] = dq.astype(jnp.bfloat16)
        dk = dot_tn(fine_ds, query[:, at]) + over_tokens(coarse_dk, cubes_whole)
        dv = dot_tn(fine_half, grad[:, at]) + over_tokens(coarse_dv, cubes_whole)
        dk, dv = dk.astype(jnp.bfloat16), dv.astype(jnp.bfloat16)
        for ctx in range(2):
            terms[ctx, head, 0] = dk[ctx * tokens : (ctx + 1) * tokens]
            terms[ctx, head, 1] = dv[ctx * tokens : (ctx + 1) * tokens]
        term_copies.append(
            send(terms.at[other, head], terms_in.at[head], term_sem, (head,), {"ctx": other})
        )

    write(query_grad, query_grad_out)

    for step in range(1, n_clip):
        turns[1][step - 1].wait_recv()
        turn_across(1, step)
    for head in range(heads):
        at = slice(head * HD, (head + 1) * HD)
        term_copies[head].wait_recv()
        summed = terms[x, head].astype(jnp.float32) + terms_in[head].astype(jnp.float32)
        key_grad[:, at] = summed[0].astype(jnp.bfloat16)
        value_grad[:, at] = summed[1].astype(jnp.bfloat16)
    write(key_grad, key_grad_out)
    write(value_grad, value_grad_out)
    for copy in turn_far[1:2] + turn_far[-(n_clip - 1) :]:
        copy.wait_recv()
    weight_rows(1)
    if relayed:
        for step in range(1, n_clip):
            pl.when(jnp.logical_not(end_to_end(step)))(turns[0][step - 1].wait_send)
        pl.when(jnp.logical_not(ends))(lambda: relay().wait_send())
    for copy in sent:
        copy.wait_send()
    for copy in written:
        copy.wait()


def copy_out(*refs):
    sem = refs[-1]
    n_out = len(refs) // 3
    loads = [
        pltpu.make_async_copy(refs[index], refs[2 * n_out + index], sem.at[0, index])
        for index in range(n_out)
    ]
    stores = [
        pltpu.make_async_copy(refs[2 * n_out + index], refs[n_out + index], sem.at[1, index])
        for index in range(n_out)
    ]
    for copy in loads:
        copy.start()
    for load, store in zip(loads, stores):
        load.wait()
        store.start()
    for copy in stores:
        copy.wait()


def paired(n_clip, n_head, queries, key_states, value_states, layer_grad, out_weight, chosen):
    tokens, width = queries.shape[1:]
    cols = out_weight.shape[1]
    heads = width // HD
    half = jnp.bfloat16
    whole = 2 * tokens
    far = pl.BlockSpec(memory_space=pltpu.HBM)
    small = jax.ShapeDtypeStruct((tokens, width), half)
    dma = pltpu.SemaphoreType.DMA
    outs = pl.pallas_call(
        functools.partial(pair_kernel, n_clip, n_head),
        out_shape=(small, small, small, small, jax.ShapeDtypeStruct((width, cols), half)),
        in_specs=[far] * 6,
        out_specs=(far,) * 5,
        scratch_shapes=[pltpu.VMEM((tokens, width), half)] * 4
        + [
            pltpu.VMEM((width, cols), half),
            pltpu.SMEM(chosen.shape[1:], jnp.int32),
            pltpu.VMEM((tokens, width), half),
            pltpu.VMEM((whole, width), half),
            pltpu.VMEM((whole, width), half),
            pltpu.VMEM((2, n_clip, tokens, cols), half),
            pltpu.VMEM((width, cols), half),
            pltpu.VMEM((cols, width), half),
            pltpu.VMEM((heads, tokens, whole), jnp.float32),
            pltpu.VMEM((heads, ROWS, ROWS), jnp.float32),
            pltpu.VMEM((width, 2 * n_clip * tokens), half),
            pltpu.VMEM((n_clip, tokens, width), half),
            pltpu.VMEM((n_clip, tokens, width), half),
            pltpu.VMEM((tokens, width), half),
            pltpu.VMEM((2, heads, 2, tokens, HD), half),
            pltpu.VMEM((heads, 2, tokens, HD), half),
            dma((2, 2)),
            dma((2, n_clip)),
            dma((2, n_clip, n_head)),
            dma((2, n_clip)),
            dma((2, n_head)),
            dma((2, n_clip)),
            dma((2, 2, n_clip)),
            dma((2, 2, n_clip)),
            dma((2, heads)),
            dma((6,)),
            dma((6,)),
        ],
        compiler_params=pltpu.CompilerParams(
            collective_id=0, has_side_effects=True, vmem_limit_bytes=60 * 2**20
        ),
    )(chosen[0], queries[0], key_states[0], value_states[0], layer_grad[0], out_weight)
    outs = pl.pallas_call(
        copy_out,
        out_shape=tuple(jax.ShapeDtypeStruct(out.shape, half) for out in outs),
        in_specs=[far] * 5,
        out_specs=(far,) * 5,
        scratch_shapes=[pltpu.VMEM(out.shape, half) for out in outs] + [dma((2, 5))],
        compiler_params=pltpu.CompilerParams(vmem_limit_bytes=60 * 2**20),
    )(*outs)
    return tuple(out[None] for out in outs[:4]) + (outs[4],)


def solution(mesh):
    clips, heads = mesh.shape["clip"], mesh.shape["head"]
    paired_here = mesh.shape["ctx"] == 2 and heads == 4
    body = functools.partial(paired, clips, heads) if paired_here else on_device
    placed = (
        P("clip", "ctx", "head"),
        P("clip", "ctx", "head"),
        P("clip", "ctx", "head"),
        P("clip", "ctx", None),
        P("head", "clip"),
        P("clip", "ctx", None),
    )
    return jax.shard_map(
        body,
        mesh=mesh,
        in_specs=placed,
        out_specs=(
            P("clip", "ctx", "head"),
            P("clip", "ctx", "head"),
            P("clip", "ctx", "head"),
            P("clip", "ctx", "head"),
            P("head", "clip"),
        ),
        check_vma=False,
    )
```

```python
import functools

import jax
import jax.numpy as jnp
from jax import lax
from jax.experimental import pallas as pl
from jax.experimental.pallas import tpu as pltpu
from jax.sharding import PartitionSpec as P

HD = 128
CUBE = 64


def cube_means(blocks):
    grouped = blocks.astype(jnp.float32).reshape(-1, CUBE, blocks.shape[-1])
    return jnp.mean(grouped, axis=1).astype(jnp.bfloat16)


def by_heads(blocks):
    return blocks.reshape(blocks.shape[0], -1, HD)


def softmax_rows(scores):
    largest = jnp.max(scores, axis=-1, keepdims=True)
    expons = jnp.exp(scores - largest)
    return expons / jnp.sum(expons, axis=-1, keepdims=True)


def on_device(queries, key_states, value_states, layer_grad, out_weight, chosen):
    scaling = HD ** (-0.5)
    query_local = queries[0]
    key_local = key_states[0]
    value_local = value_states[0]
    layer_local = layer_grad[0]
    picked = chosen[0]
    tok_local, width = query_local.shape
    heads_here = width // HD
    cubes_local = tok_local // CUBE
    picks_each = picked.shape[1]
    kv_whole = lax.all_gather(
        jnp.concatenate([key_local, value_local], axis=1), "ctx", axis=0, tiled=True
    )
    key_whole, value_whole = kv_whole[:, :width], kv_whole[:, width:]
    columns = lax.all_to_all(layer_local, "clip", split_axis=1, concat_axis=0, tiled=True)
    grad_parts = lax.dot_general(
        columns, out_weight, (((1,), (1,)), ((), ())), preferred_element_type=jnp.float32
    ).astype(jnp.bfloat16)
    grad_parts = lax.all_to_all(
        grad_parts.reshape(-1, tok_local, width), "clip", split_axis=0, concat_axis=0, tiled=True
    )
    attn_grad = jnp.sum(grad_parts.astype(jnp.float32), axis=0).astype(jnp.bfloat16)
    columns_whole = lax.all_gather(columns, "ctx", axis=0, tiled=True)
    tok_whole = key_whole.shape[0]
    cubes_whole = tok_whole // CUBE
    query_cube = cube_means(query_local)
    key_cube, value_cube = cube_means(key_whole), cube_means(value_whole)
    qcube_heads = by_heads(query_cube)
    kcube_heads = by_heads(key_cube)
    vcube_heads = by_heads(value_cube)
    coarse_scores = (
        jnp.einsum("ahd,bhd->hab", qcube_heads, kcube_heads, preferred_element_type=jnp.float32)
        * scaling
    )
    coarse_p = softmax_rows(coarse_scores)
    coarse_half = coarse_p.astype(jnp.bfloat16)
    coarse_out = jnp.einsum(
        "hab,bhd->ahd", coarse_half, vcube_heads, preferred_element_type=jnp.float32
    )
    key_cubes = key_whole.reshape(cubes_whole, CUBE, width)
    value_cubes = value_whole.reshape(cubes_whole, CUBE, width)
    key_pick = key_cubes[picked].reshape(cubes_local, picks_each * CUBE, heads_here, HD)
    value_pick = value_cubes[picked].reshape(cubes_local, picks_each * CUBE, heads_here, HD)
    query_blocks = query_local.reshape(cubes_local, CUBE, heads_here, HD)
    fine_scores = (
        jnp.einsum("cthd,ckhd->chtk", query_blocks, key_pick, preferred_element_type=jnp.float32)
        * scaling
    )
    fine_p = softmax_rows(fine_scores)
    fine_half = fine_p.astype(jnp.bfloat16)
    fine_out = jnp.einsum(
        "chtk,ckhd->cthd", fine_half, value_pick, preferred_element_type=jnp.float32
    )
    attention = (
        (fine_out + coarse_out[:, None, :, :]).astype(jnp.bfloat16).reshape(tok_local, width)
    )
    attention_whole = lax.all_gather(attention, ("ctx", "clip"), axis=0, tiled=True)
    grad_cube = jnp.sum(
        attn_grad.astype(jnp.float32).reshape(cubes_local, CUBE, width), axis=1
    ).astype(jnp.bfloat16)
    gcube_heads = by_heads(grad_cube)
    coarse_dp = jnp.einsum(
        "ahd,bhd->hab", gcube_heads, vcube_heads, preferred_element_type=jnp.float32
    )
    coarse_delta = jnp.sum(coarse_p * coarse_dp, axis=-1, keepdims=True)
    coarse_ds = (scaling * coarse_p * (coarse_dp - coarse_delta)).astype(jnp.bfloat16)
    coarse_dq = jnp.einsum(
        "hab,bhd->ahd", coarse_ds, kcube_heads, preferred_element_type=jnp.float32
    )
    coarse_dk = jnp.einsum(
        "hab,ahd->bhd", coarse_ds, qcube_heads, preferred_element_type=jnp.float32
    )
    coarse_dv = jnp.einsum(
        "hab,ahd->bhd", coarse_half, gcube_heads, preferred_element_type=jnp.float32
    )
    cube_terms = (
        jnp.concatenate(
            [coarse_dk.reshape(cubes_whole, width), coarse_dv.reshape(cubes_whole, width)], axis=1
        )
        / CUBE
    )
    grad_blocks = attn_grad.reshape(cubes_local, CUBE, heads_here, HD)
    fine_dp = jnp.einsum(
        "cthd,ckhd->chtk", grad_blocks, value_pick, preferred_element_type=jnp.float32
    )
    fine_delta = jnp.sum(fine_p * fine_dp, axis=-1, keepdims=True)
    fine_ds = (scaling * fine_p * (fine_dp - fine_delta)).astype(jnp.bfloat16)
    query_grad = jnp.einsum(
        "chtk,ckhd->cthd", fine_ds, key_pick, preferred_element_type=jnp.float32
    )
    query_grad = (query_grad + coarse_dq[:, None, :, :] / CUBE).astype(jnp.bfloat16)
    query_grad = query_grad.reshape(tok_local, width)
    key_picked = jnp.einsum(
        "chtk,cthd->ckhd", fine_ds, query_blocks, preferred_element_type=jnp.float32
    )
    value_picked = jnp.einsum(
        "chtk,cthd->ckhd", fine_half, grad_blocks, preferred_element_type=jnp.float32
    )
    flat_terms = jnp.concatenate(
        [
            key_picked.reshape(cubes_local, picks_each, CUBE, width),
            value_picked.reshape(cubes_local, picks_each, CUBE, width),
        ],
        axis=3,
    )
    flat_terms = flat_terms.reshape(cubes_local * picks_each, CUBE, 2 * width)
    picked_flat = picked.reshape(-1)
    running = jnp.broadcast_to(cube_terms[:, None, :], (cubes_whole, CUBE, 2 * width))
    running = running.at[picked_flat].add(flat_terms)
    summed = lax.psum_scatter(
        running.reshape(tok_whole, 2 * width).astype(jnp.bfloat16),
        "ctx",
        scatter_dimension=0,
        tiled=True,
    ).astype(jnp.float32)
    key_grad = summed[:, :width].astype(jnp.bfloat16)
    value_grad = summed[:, width:].astype(jnp.bfloat16)
    weight_grad = lax.dot_general(
        attention_whole, columns_whole, (((0,), (0,)), ((), ())), preferred_element_type=jnp.float32
    ).astype(jnp.bfloat16)
    return (attention[None], query_grad[None], key_grad[None], value_grad[None], weight_grad)

ROWS = 16
LOW = -1e30


def dot_nt(a, b):
    return lax.dot_general(a, b, (((1,), (1,)), ((), ())), preferred_element_type=jnp.float32)


def dot_nn(a, b):
    return lax.dot_general(a, b, (((1,), (0,)), ((), ())), preferred_element_type=jnp.float32)


def dot_tn(a, b):
    return lax.dot_general(a, b, (((0,), (0,)), ((), ())), preferred_element_type=jnp.float32)


def cube_rows(blocks, factor):
    at_row = lax.broadcasted_iota(jnp.int32, (ROWS, blocks.shape[1]), 0)
    rows = jnp.zeros((ROWS, blocks.shape[1]), jnp.float32)
    for cube in range(blocks.shape[0] // CUBE):
        part = blocks[cube * CUBE : (cube + 1) * CUBE].astype(jnp.float32)
        total = jnp.sum(part, axis=0, keepdims=True) * factor
        rows = jnp.where(at_row == cube, total, rows)
    return rows.astype(jnp.bfloat16)


def over_tokens(rows, cubes):
    return jnp.concatenate(
        [jnp.broadcast_to(rows[cube : cube + 1], (CUBE, rows.shape[1])) for cube in range(cubes)],
        axis=0,
    )


def pair_kernel(
    n_clip, n_head, chosen_in, query_in, key, value, layer, weight,
    attention_out, query_grad_out, key_grad_out, value_grad_out, weight_grad_out,
    attention, query_grad, key_grad, value_grad, weight_grad, chosen, query, keys, values, columns, held_weight, weight_t, fine, coarse, turned,
    partial, partial_in, grad, terms, terms_in,
    kv_sem, deal_sem, share_sem, across_sem, share_far_sem, part_sem, turn_sem, turn_far_sem,
    term_sem, local_sem, out_sem,
):
    scaling = HD ** (-0.5)
    tokens, width = query_in.shape
    cols = weight.shape[1]
    heads = width // HD
    cubes = tokens // CUBE
    cubes_whole = 2 * cubes
    quarter = tokens // n_head
    x, h, z = lax.axis_index("ctx"), lax.axis_index("head"), lax.axis_index("clip")
    other = 1 - x
    near, over = h + 1 - 2 * lax.rem(h, 2), lax.rem(h + 2, n_head)

    def rows_of(head):
        return pl.ds(pl.multiple_of(head * quarter, quarter), quarter)

    my_rows, over_rows = rows_of(h), rows_of(over)

    def to_clip(step):
        return {"clip": lax.rem(z + step, n_clip)}

    def from_clip(step):
        return lax.rem(z + n_clip - step, n_clip)

    def column_block(clip):
        return pl.ds(pl.multiple_of(clip * cols, cols), cols)

    def slot(ctx, clip):
        return pl.ds(pl.multiple_of((ctx * n_clip + clip) * tokens, tokens), tokens)

    sent, written = [], []

    def write(src, dst):
        copy = pltpu.make_async_copy(src, dst, out_sem.at[len(written)])
        copy.start()
        written.append(copy)

    def send(src, dst, sems, index, device):
        copy = pltpu.make_async_remote_copy(
            src_ref=src, dst_ref=dst,
            send_sem=sems.at[(0,) + index], recv_sem=sems.at[(1,) + index],
            device_id=device, device_id_type=pl.DeviceIdType.MESH,
        )
        copy.start()
        sent.append(copy)
        return copy

    mine = pl.ds(pl.multiple_of(x * tokens, tokens), tokens)
    locals_in = [
        pltpu.make_async_copy(src, dst, local_sem.at[index])
        for index, (src, dst) in enumerate(
            [
                (query_in, query),
                (key, keys.at[mine]),
                (value, values.at[mine]),
                (weight, held_weight),
                (layer.at[:, column_block(z)], columns.at[x, z]),
                (chosen_in, chosen),
            ]
        )
    ]
    for copy in locals_in:
        copy.start()

    barrier = pltpu.get_barrier_semaphore()
    partners = [{"ctx": other}]
    partners += [to_clip(step) for step in range(1, n_clip)]
    partners += [{"head": near}, {"head": over}]
    for partner in partners:
        pl.semaphore_signal(barrier, inc=1, device_id=partner, device_id_type=pl.DeviceIdType.MESH)
    pl.semaphore_wait(barrier, len(partners))

    key_copy = send(key, keys.at[mine], kv_sem, (0,), {"ctx": other})
    value_copy = send(value, values.at[mine], kv_sem, (1,), {"ctx": other})
    deals = [None]
    for step in range(1, n_clip):
        deals.append(
            send(
                layer.at[my_rows, column_block(lax.rem(z + step, n_clip))],
                columns.at[x, z, my_rows], deal_sem, (step,), to_clip(step),
            )
        )
    across = [
        send(
            layer.at[my_rows, column_block(z)], columns.at[x, z, my_rows],
            across_sem, (0,), {"ctx": other},
        )
    ]
    for copy in locals_in:
        copy.wait()
    for head in range(heads):
        at = slice(head * HD, (head + 1) * HD)
        weight_t[:, at] = held_weight[at, :].T
    query_cube = cube_rows(query[...], 1.0 / CUBE)
    column_cube = lax.broadcasted_iota(jnp.int32, (1, cubes_whole * CUBE), 1) // CUBE
    allowed = []
    for cube in range(cubes):
        hit = column_cube == chosen[cube, 0]
        for pick in range(1, chosen.shape[1]):
            hit = hit | (column_cube == chosen[cube, pick])
        allowed.append(jnp.broadcast_to(hit.astype(jnp.float32), (CUBE, cubes_whole * CUBE)))
    allowed = jnp.concatenate(allowed, axis=0) > 0.5
    real = lax.broadcasted_iota(jnp.int32, (ROWS, ROWS), 1) < cubes_whole

    shares = [None]

    def pass_on(step):
        deals[step].wait_recv()
        piece = columns.at[x, from_clip(step), my_rows]
        shares.append(
            [
                send(piece, piece, share_sem, (step, 0), {"head": over}),
                send(piece, piece, share_sem, (step, 1), {"head": near}),
            ]
        )
        across.append(send(piece, piece, across_sem, (step,), {"ctx": other}))

    def hand_on(step):
        shares[step][0].wait_recv()
        piece = columns.at[x, from_clip(step), over_rows]
        shares[step].append(send(piece, piece, share_sem, (step, 2), {"head": near}))

    key_copy.wait_recv()
    key_cube = cube_rows(keys[...], 1.0 / CUBE)
    for head in range(heads):
        at = slice(head * HD, (head + 1) * HD)
        scores = dot_nt(query[:, at], keys[:, at]) * scaling
        scores = jnp.where(allowed, scores, LOW)
        expons = jnp.exp(scores - jnp.max(scores, axis=-1, keepdims=True))
        fine[head] = expons / jnp.sum(expons, axis=-1, keepdims=True)
        coarse_scores = dot_nt(query_cube[:, at], key_cube[:, at]) * scaling
        coarse_scores = jnp.where(real, coarse_scores, LOW)
        expons = jnp.exp(coarse_scores - jnp.max(coarse_scores, axis=-1, keepdims=True))
        coarse[head] = expons / jnp.sum(expons, axis=-1, keepdims=True)

    for step in range(1, n_clip):
        pass_on(step)
    value_copy.wait_recv()
    value_cube = cube_rows(values[...], 1.0 / CUBE)

    early = heads - 1
    split = (slice(0, early * HD), slice(early * HD, width))
    turns, turn_far = [], []

    def turn_out(part):
        piece = turned.at[split[part], slot(x, z)]
        turns.append(
            [send(piece, piece, turn_sem, (part, step), to_clip(step)) for step in range(1, n_clip)]
        )

    def turn_across(part, step):
        piece = turned.at[split[part], slot(x, from_clip(step))]
        turn_far.append(send(piece, piece, turn_far_sem, (part, step), {"ctx": other}))

    for head in range(heads):
        at = slice(head * HD, (head + 1) * HD)
        coarse_out = dot_nn(coarse[head].astype(jnp.bfloat16), value_cube[:, at])
        fine_out = dot_nn(fine[head].astype(jnp.bfloat16), values[:, at])
        result = (fine_out + over_tokens(coarse_out, cubes)).astype(jnp.bfloat16)
        attention[:, at] = result
        turned[at, slot(x, z)] = result.astype(jnp.float32).T.astype(jnp.bfloat16)
        if head == early - 1:
            turn_out(0)
            turn_across(0, 0)
        if head == heads // 2:
            for step in range(1, n_clip):
                hand_on(step)
    turn_across(1, 0)
    write(attention, attention_out)

    parts = [None]
    for step in range(1, n_clip):
        clip = from_clip(step)
        for copy in shares[step][1:]:
            copy.wait_recv()
        partial[step] = dot_nn(columns[x, clip], weight_t[...]).astype(jnp.bfloat16)
        parts.append(
            send(
                partial.at[step], partial_in.at[step], part_sem, (step,),
                {"clip": clip},
            )
        )
    total = dot_nn(columns[x, z], weight_t[...])
    for copy in across:
        copy.wait_recv()
    far = columns.at[other, :, my_rows]
    share_far = [
        send(far, far, share_far_sem, (0,), {"head": over}),
        send(far, far, share_far_sem, (1,), {"head": near}),
    ]
    for step in range(1, n_clip):
        turns[0][step - 1].wait_recv()
        turn_across(0, step)

    def weight_rows(part):
        for begin in range(0, cols, tile):
            at = slice(begin, begin + tile)
            block = columns[:, :, :, at].reshape(2 * n_clip * tokens, tile)
            weight_grad[split[part], at] = dot_nn(turned[split[part], :], block).astype(jnp.bfloat16)
        write(weight_grad.at[split[part]], weight_grad_out.at[split[part]])

    tile = 256
    for step in range(1, n_clip):
        parts[step].wait_recv()
        total = total + partial_in[step].astype(jnp.float32)
    turn_out(1)
    grad[...] = total.astype(jnp.bfloat16)
    share_far[0].wait_recv()
    far = columns.at[other, :, over_rows]
    share_far.append(send(far, far, share_far_sem, (2,), {"head": near}))
    grad_cube = cube_rows(grad[...], 1.0)

    term_copies = []
    for head in range(heads):
        at = slice(head * HD, (head + 1) * HD)
        fine_p = fine[head]
        fine_half = fine_p.astype(jnp.bfloat16)
        fine_dp = dot_nt(grad[:, at], values[:, at])
        delta = jnp.sum(fine_p * fine_dp, axis=-1, keepdims=True)
        fine_ds = (scaling * fine_p * (fine_dp - delta)).astype(jnp.bfloat16)
        coarse_p = coarse[head]
        coarse_half = coarse_p.astype(jnp.bfloat16)
        coarse_dp = dot_nt(grad_cube[:, at], value_cube[:, at])
        delta = jnp.sum(coarse_p * coarse_dp, axis=-1, keepdims=True)
        coarse_ds = (scaling * coarse_p * (coarse_dp - delta)).astype(jnp.bfloat16)
        coarse_dq = dot_nn(coarse_ds, key_cube[:, at]) * (1.0 / CUBE)
        coarse_dk = dot_tn(coarse_ds, query_cube[:, at]) * (1.0 / CUBE)
        coarse_dv = dot_tn(coarse_half, grad_cube[:, at]) * (1.0 / CUBE)
        dq = dot_nn(fine_ds, keys[:, at]) + over_tokens(coarse_dq, cubes)
        query_grad[:, at] = dq.astype(jnp.bfloat16)
        dk = dot_tn(fine_ds, query[:, at]) + over_tokens(coarse_dk, cubes_whole)
        dv = dot_tn(fine_half, grad[:, at]) + over_tokens(coarse_dv, cubes_whole)
        dk, dv = dk.astype(jnp.bfloat16), dv.astype(jnp.bfloat16)
        for ctx in range(2):
            terms[ctx, head, 0] = dk[ctx * tokens : (ctx + 1) * tokens]
            terms[ctx, head, 1] = dv[ctx * tokens : (ctx + 1) * tokens]
        term_copies.append(
            send(terms.at[other, head], terms_in.at[head], term_sem, (head,), {"ctx": other})
        )

    write(query_grad, query_grad_out)
    for copy in share_far[1:] + turn_far[:1] + turn_far[2:]:
        copy.wait_recv()
    for step in range(1, n_clip):
        turns[1][step - 1].wait_recv()
        turn_across(1, step)
    weight_rows(0)

    for head in range(heads):
        at = slice(head * HD, (head + 1) * HD)
        term_copies[head].wait_recv()
        summed = terms[x, head].astype(jnp.float32) + terms_in[head].astype(jnp.float32)
        key_grad[:, at] = summed[0].astype(jnp.bfloat16)
        value_grad[:, at] = summed[1].astype(jnp.bfloat16)
    write(key_grad, key_grad_out)
    write(value_grad, value_grad_out)
    for copy in turn_far[1:2] + turn_far[-(n_clip - 1) :]:
        copy.wait_recv()
    weight_rows(1)
    for copy in sent:
        copy.wait_send()
    for copy in written:
        copy.wait()


def copy_out(*refs):
    sem = refs[-1]
    n_out = len(refs) // 3
    loads = [
        pltpu.make_async_copy(refs[index], refs[2 * n_out + index], sem.at[0, index])
        for index in range(n_out)
    ]
    stores = [
        pltpu.make_async_copy(refs[2 * n_out + index], refs[n_out + index], sem.at[1, index])
        for index in range(n_out)
    ]
    for copy in loads:
        copy.start()
    for load, store in zip(loads, stores):
        load.wait()
        store.start()
    for copy in stores:
        copy.wait()


def paired(n_clip, n_head, queries, key_states, value_states, layer_grad, out_weight, chosen):
    tokens, width = queries.shape[1:]
    cols = out_weight.shape[1]
    heads = width // HD
    half = jnp.bfloat16
    whole = 2 * tokens
    far = pl.BlockSpec(memory_space=pltpu.HBM)
    small = jax.ShapeDtypeStruct((tokens, width), half)
    dma = pltpu.SemaphoreType.DMA
    outs = pl.pallas_call(
        functools.partial(pair_kernel, n_clip, n_head),
        out_shape=(small, small, small, small, jax.ShapeDtypeStruct((width, cols), half)),
        in_specs=[far] * 6,
        out_specs=(far,) * 5,
        scratch_shapes=[pltpu.VMEM((tokens, width), half)] * 4
        + [
            pltpu.VMEM((width, cols), half),
            pltpu.SMEM(chosen.shape[1:], jnp.int32),
            pltpu.VMEM((tokens, width), half),
            pltpu.VMEM((whole, width), half),
            pltpu.VMEM((whole, width), half),
            pltpu.VMEM((2, n_clip, tokens, cols), half),
            pltpu.VMEM((width, cols), half),
            pltpu.VMEM((cols, width), half),
            pltpu.VMEM((heads, tokens, whole), jnp.float32),
            pltpu.VMEM((heads, ROWS, ROWS), jnp.float32),
            pltpu.VMEM((width, 2 * n_clip * tokens), half),
            pltpu.VMEM((n_clip, tokens, width), half),
            pltpu.VMEM((n_clip, tokens, width), half),
            pltpu.VMEM((tokens, width), half),
            pltpu.VMEM((2, heads, 2, tokens, HD), half),
            pltpu.VMEM((heads, 2, tokens, HD), half),
            dma((2, 2)),
            dma((2, n_clip)),
            dma((2, n_clip, n_head)),
            dma((2, n_clip)),
            dma((2, n_head)),
            dma((2, n_clip)),
            dma((2, 2, n_clip)),
            dma((2, 2, n_clip)),
            dma((2, heads)),
            dma((6,)),
            dma((6,)),
        ],
        compiler_params=pltpu.CompilerParams(
            collective_id=0, has_side_effects=True, vmem_limit_bytes=60 * 2**20
        ),
    )(chosen[0], queries[0], key_states[0], value_states[0], layer_grad[0], out_weight)
    outs = pl.pallas_call(
        copy_out,
        out_shape=tuple(jax.ShapeDtypeStruct(out.shape, half) for out in outs),
        in_specs=[far] * 5,
        out_specs=(far,) * 5,
        scratch_shapes=[pltpu.VMEM(out.shape, half) for out in outs] + [dma((2, 5))],
        compiler_params=pltpu.CompilerParams(vmem_limit_bytes=60 * 2**20),
    )(*outs)
    return tuple(out[None] for out in outs[:4]) + (outs[4],)


def solution(mesh):
    clips, heads = mesh.shape["clip"], mesh.shape["head"]
    paired_here = mesh.shape["ctx"] == 2 and heads == 4
    body = functools.partial(paired, clips, heads) if paired_here else on_device
    placed = (
        P("clip", "ctx", "head"),
        P("clip", "ctx", "head"),
        P("clip", "ctx", "head"),
        P("clip", "ctx", None),
        P("head", "clip"),
        P("clip", "ctx", None),
    )
    return jax.shard_map(
        body,
        mesh=mesh,
        in_specs=placed,
        out_specs=(
            P("clip", "ctx", "head"),
            P("clip", "ctx", "head"),
            P("clip", "ctx", "head"),
            P("clip", "ctx", "head"),
            P("head", "clip"),
        ),
        check_vma=False,
    )
```
